256 devices in a mesh: seq: 64 (over y, z, x_hi), head: 4 (over x_lo, core).
Axes of the slice: x: 4 (x_hi: 2, x_lo: 2; x = x_hi * 2 + x_lo), y: 4, z: 8, core: 2. Of those that a mesh axis runs over, the one named last changes fastest.
Arguments:
- hidden_in: bfloat16 [12288, 2048], P('seq', 'head'), may hold values from -6 to 6
- delta_q: bfloat16 [12288, 2048], P('seq', 'head'), may hold values from -6 to 6
- delta_k: bfloat16 [12288, 2048], P('seq', 'head'), may hold values from -6 to 6
- delta_v: bfloat16 [12288, 2048], P('seq', 'head'), may hold values from -6 to 6
- beta: float32 [12288, 16], P('seq', 'head'), may hold values from 0.002 to 0.02
- log_decay: float32 [12288, 16], P('seq', 'head'), may hold values from -1 to 0
- resets: int32 [12288], P('seq'), may hold values from 0 to 1, as said below
- attn_q: bfloat16 [12288, 2048], P('seq', 'head'), may hold values from -5.5 to 5.5
- attn_k: bfloat16 [12288, 2048], P('seq', 'head'), may hold values from -5.5 to 5.5
- attn_v: bfloat16 [12288, 2048], P('seq', 'head'), may hold values from -6 to 6
- delta_gain: float32 [128], replicated, may hold values from 0.5 to 1.5
- attn_gain: float32 [128], replicated, may hold values from 0.5 to 1.5
- out_weight: bfloat16 [2048, 2048], P('head'), may hold values from -0.125 to 0.125
Outputs:
- mixed: bfloat16 [12288, 2048], P('seq', 'head')
The draws below stay inside these ranges and needn't reach their ends.
Inputs may be any that keep to these rules, and one draw needn't show every extreme that they name: `resets`: exactly three ones, one in each of the first three runs of 4096 tokens, never at the first token of a run.
All inputs are finite; a program needn't handle non-finite values.
Results may differ from the reference program's by a relative error of at most 0.013.
Values may be sent and summed in bfloat16 or wider, within the bound.
A program may use at most 256 MiB of HBM per device.

```python
import math
import jax
import jax.numpy as jnp
from jax import lax

D = 2048
HEADS = 16
HEAD_DIM = 128
CONTEXT_WORDS = 12288


def draw_attn_q(key, part):
    key = jax.random.fold_in(key, 21)
    random_entries = jnp.clip(jax.random.normal(key, (CONTEXT_WORDS, HEADS * HEAD_DIM), jnp.float32), -5.5, 5.5)
    return random_entries.astype(jnp.bfloat16)


def draw_attn_k(key, part):
    key = jax.random.fold_in(key, 22)
    random_entries = jnp.clip(jax.random.normal(key, (CONTEXT_WORDS, HEADS * HEAD_DIM), jnp.float32), -5.5, 5.5)
    return random_entries.astype(jnp.bfloat16)


def draw_log_decay(key, part):
    key = jax.random.fold_in(key, 11)
    slow_key, factor_key, place_key, amount_key = jax.random.split(key, 4)
    slow_share = 0.5
    lagging_channels = jax.random.bernoulli(slow_key, slow_share, (HEADS,))
    default_frequency = jnp.where(lagging_channels, math.log(10.0) / (16.0 * CONTEXT_WORDS), 1.0 / 40.0)
    multiplier_coefficient = jnp.exp(jax.random.uniform(factor_key, (CONTEXT_WORDS, HEADS), jnp.float32, -math.log(2.0), math.log(2.0)))
    index_array = jax.random.randint(place_key, (3,), 0, CONTEXT_WORDS)
    spike_duration = jnp.any(jnp.arange(CONTEXT_WORDS)[:, None] == index_array[None, :], axis=1)
    draw_amount = jax.random.uniform(amount_key, (CONTEXT_WORDS, HEADS), jnp.float32, math.log(0.6), math.log(0.8))
    random_entries = -default_frequency[None, :] * multiplier_coefficient + jnp.where(spike_duration[:, None] & lagging_channels[None, :], draw_amount, 0.0)
    return random_entries.astype(jnp.float32)


def draw_resets(key, part):
    key = jax.random.fold_in(key, 5)
    third_len = CONTEXT_WORDS // 3
    offsets = jax.random.randint(key, (3,), 1, third_len)
    index_array = jnp.arange(3) * third_len + offsets
    return jnp.any(jnp.arange(CONTEXT_WORDS)[:, None] == index_array[None, :], axis=1).astype(jnp.int32)


def steps_of(rng, dims, pieces, smallest, high):
    loudness = 1.0
    for position, shards_of in pieces:
        steps = jax.random.uniform(jax.random.fold_in(jax.random.fold_in(rng, 6), position), (shards_of,), jnp.float32, smallest / len(pieces), high / len(pieces))
        loudness = loudness * jnp.repeat(jnp.exp(steps), dims[position] // shards_of).reshape((-1,) + (1,) * (len(dims) - 1 - position))
    return loudness


def bell_draw(rng, extent, width, reach, cuts=(), kind=jnp.bfloat16):
    entries = jax.random.normal(rng, extent, jnp.float32) * width
    if len(cuts) > 0:
        entries = steps_of(rng, extent, cuts, -0.22, 0.18) * entries
    return jnp.clip(entries, min=-reach, max=reach).astype(kind)


def setup_inputs(seed: int = 0) -> dict:
    streams_of = jax.random.split(jax.random.key(seed), 14)
    return {
        "hidden_in": bell_draw(streams_of[0], (CONTEXT_WORDS, D), 1.0, 6.0, ((0, 64), (1, 4))),
        "delta_q": bell_draw(streams_of[1], (CONTEXT_WORDS, HEADS * HEAD_DIM), 1.0, 6.0, ((0, 64), (1, 4))),
        "delta_k": bell_draw(streams_of[2], (CONTEXT_WORDS, HEADS * HEAD_DIM), 1.0, 6.0, ((0, 64), (1, 4))),
        "delta_v": bell_draw(streams_of[3], (CONTEXT_WORDS, HEADS * HEAD_DIM), 1.0, 6.0, ((0, 64), (1, 4))),
        "beta": jnp.clip(jnp.exp(math.log(0.02) - 2.30258502 * jax.random.uniform(streams_of[4], (CONTEXT_WORDS, HEADS), jnp.float32) ** steps_of(streams_of[4], (CONTEXT_WORDS, HEADS), ((0, 64), (1, 4)), -0.2, 0.2)), 0.002, 0.02),
        "log_decay": draw_log_decay(jax.random.fold_in(streams_of[13], 71), 0),
        "resets": draw_resets(jax.random.fold_in(streams_of[13], 71), 0),
        "attn_q": draw_attn_q(jax.random.fold_in(streams_of[13], 71), 0),
        "attn_k": draw_attn_k(jax.random.fold_in(streams_of[13], 71), 0),
        "attn_v": bell_draw(streams_of[9], (CONTEXT_WORDS, HEADS * HEAD_DIM), 1.0, 6.0, ((0, 64), (1, 4))),
        "delta_gain": jnp.clip(1.0 + 0.1 * jax.random.normal(streams_of[10], (HEAD_DIM,), jnp.float32), 0.5, 1.5),
        "attn_gain": jnp.clip(1.0 + 0.1 * jax.random.normal(streams_of[11], (HEAD_DIM,), jnp.float32), 0.5, 1.5),
        "out_weight": bell_draw(streams_of[12], (HEADS * HEAD_DIM, D), (HEADS * HEAD_DIM) ** -0.5, 0.125, ((0, 4),)),
    }


HIGHEST_MODE = lax.Precision.HIGHEST
EPSILON = 1e-06

def unit_rows(tensor):
    return tensor * lax.rsqrt(lax.optimization_barrier(jnp.sum(tensor * tensor, axis=-1, keepdims=True)) + EPSILON)

def rms_scaled(tensor, scales):
    return tensor * lax.rsqrt(lax.optimization_barrier(jnp.mean(tensor * tensor, axis=-1, keepdims=True)) + EPSILON) * scales

def reference(hidden_in, delta_q, delta_k, delta_v, beta, log_decay, resets, attn_q, attn_k, attn_v, delta_gain, attn_gain, out_weight):
    queries = unit_rows(delta_q.astype(jnp.float32).reshape(CONTEXT_WORDS, HEADS, HEAD_DIM)) * HEAD_DIM ** (-0.5)
    keys_unit = unit_rows(delta_k.astype(jnp.float32).reshape(CONTEXT_WORDS, HEADS, HEAD_DIM))
    values = delta_v.astype(jnp.float32).reshape(CONTEXT_WORDS, HEADS, HEAD_DIM)
    keep_rate = jnp.exp(log_decay) * (1.0 - resets.astype(jnp.float32))[:, None]

    def advance(state, inputs):
        query_t, key_t, value_t, beta_t, keep_t = inputs
        probe = jnp.einsum('hvk,hk->hv', state, key_t, precision=HIGHEST_MODE)
        erased = state - beta_t[:, None, None] * probe[:, :, None] * key_t[:, None, :]
        state = keep_t[:, None, None] * erased + beta_t[:, None, None] * value_t[:, :, None] * key_t[:, None, :]
        return (state, jnp.einsum('hvk,hk->hv', state, query_t, precision=HIGHEST_MODE))
    start_state = jnp.zeros((HEADS, HEAD_DIM, HEAD_DIM), jnp.float32)
    _, delta_raw = lax.scan(advance, start_state, (queries, keys_unit, values, beta, keep_rate))
    delta_normed = rms_scaled(delta_raw, delta_gain)
    block_rows = math.gcd(CONTEXT_WORDS, 256)
    attn_keys = attn_k.astype(jnp.float32).reshape(CONTEXT_WORDS, HEADS, HEAD_DIM)
    attn_values = attn_v.astype(jnp.float32).reshape(CONTEXT_WORDS, HEADS, HEAD_DIM)
    key_pos = jnp.arange(CONTEXT_WORDS, dtype=jnp.int32)

    def one_block(index):
        start = index.astype(jnp.int32) * block_rows
        query_rows = lax.dynamic_slice_in_dim(attn_q, start, block_rows, 0).astype(jnp.float32)
        query_rows = query_rows.reshape(block_rows, HEADS, HEAD_DIM)
        scores = jnp.einsum('qhe,khe->hqk', query_rows, attn_keys) * HEAD_DIM ** (-0.5)
        query_pos = start + jnp.arange(block_rows, dtype=jnp.int32)
        visible = key_pos[None, :] <= query_pos[:, None]
        scores = jnp.where(visible[None], scores, -jnp.inf)
        row_peak = lax.optimization_barrier(jnp.max(scores, axis=-1, keepdims=True))
        weights = jnp.exp(scores - row_peak)
        rounded = lax.optimization_barrier(weights.astype(jnp.bfloat16)).astype(jnp.float32)
        weight_sum = lax.optimization_barrier(jnp.sum(weights, axis=-1)).transpose(1, 0)
        summed = jnp.einsum('hqk,khe->qhe', rounded, attn_values)
        return summed / weight_sum[:, :, None]
    attn_raw = lax.map(one_block, jnp.arange(CONTEXT_WORDS // block_rows, dtype=jnp.int32))
    attn_raw = attn_raw.reshape(CONTEXT_WORDS, HEADS, HEAD_DIM)
    attn_normed = rms_scaled(attn_raw, attn_gain)
    combined = (0.5 * (delta_normed + attn_normed)).reshape(CONTEXT_WORDS, HEADS * HEAD_DIM).astype(jnp.bfloat16)
    branch = jnp.dot(combined, out_weight, preferred_element_type=jnp.float32)
    return (hidden_in.astype(jnp.float32) + branch).astype(jnp.bfloat16)
```

```python
import jax
import jax.numpy as jnp
from jax import lax
from jax.experimental import pallas as pl
from jax.experimental.pallas import tpu as pltpu
from jax.sharding import PartitionSpec as P

HD = 128
EPSILON = 1e-06
NY, NZ, NX = 4, 8, 2
HEADS = 4
GROUP = 4
SUB = 64
MESH = pl.DeviceIdType.MESH
HIGHEST = lax.Precision.HIGHEST
F32 = jnp.float32
BF16 = jnp.bfloat16
NEG = -1e30
SCALE = HD**-0.5
LOG2E = 1.4426950408889634
Y_ORDER = (0, 1, 3, 2)
UP_HOPS = (4, 4, 3, 3)
DOWN_HOPS = (3, 3, 4, 4)


def mm(a, b):
    return jnp.dot(a.astype(BF16), b.astype(BF16), preferred_element_type=F32)


def mm_nt(a, b, precision=None):
    return lax.dot_general(
        a, b, (((1,), (1,)), ((), ())), precision=precision, preferred_element_type=F32
    )


def mm_tn(a, b):
    return lax.dot_general(
        a.astype(BF16), b.astype(BF16), (((0,), (0,)), ((), ())), preferred_element_type=F32
    )


def place():
    s = lax.axis_index("seq")
    return s // (NZ * NX), (s // NX) % NZ, s % NX


def at(y, z, x):
    return {"seq": ((y % NY) * NZ + z % NZ) * NX + x % NX}


def remote(src, dst, send, recv, device):
    return pltpu.make_async_remote_copy(
        src_ref=src,
        dst_ref=dst,
        send_sem=send,
        recv_sem=recv,
        device_id=device,
        device_id_type=MESH,
    )


def delta_head(h, dq, dk, dv, beta, cum_col, cum_row, low, oloc, qeff, ab_send):
    tokens = dq.shape[0]
    col = slice(h * HD, (h + 1) * HD)
    q = dq[:, col].astype(F32)
    k = dk[:, col].astype(F32)
    v = dv[:, col].astype(F32)
    q = q * (lax.rsqrt(jnp.sum(q * q, axis=-1, keepdims=True) + EPSILON) * SCALE)
    k = k * lax.rsqrt(jnp.sum(k * k, axis=-1, keepdims=True) + EPSILON)
    strength = beta[:, h : h + 1]
    row_id = lax.broadcasted_iota(jnp.int32, (tokens, tokens), 0)
    col_id = lax.broadcasted_iota(jnp.int32, (tokens, tokens), 1)
    c_col, n_col = cum_col[:, h : h + 1], cum_col[:, HEADS : HEADS + 1]
    c_row, n_row = cum_row[h : h + 1, :], cum_row[HEADS : HEADS + 1, :]
    reach = jnp.where(n_col < 0.5, jnp.exp(c_col), 0.0)
    same = (jnp.abs(n_col - n_row) < 0.5) & (row_id >= col_id)
    ratios = jnp.where(same, jnp.exp(jnp.minimum(c_col - c_row, 0.0)), 0.0)
    kb = k.astype(BF16)
    inner = mm_nt(kb, kb)
    system = jnp.where(row_id > col_id, strength * ratios * inner, 0.0)
    near = (row_id // SUB) == (col_id // SUB)
    power = jnp.where(near, -system, 0.0)
    far = jnp.where(near, 0.0, system)
    inverse = jnp.where(row_id == col_id, 1.0, power)
    reached = 2
    while reached < SUB:
        power = mm(power, power)
        inverse = inverse + mm(inverse, power)
        reached *= 2
    right = jnp.concatenate([strength * v, (strength * reach) * k], axis=1)
    solved = mm(inverse, right)
    spread = mm(inverse, far)
    total = solved
    for _ in range((tokens + SUB - 1) // SUB - 1):
        total = solved - mm(spread, total)
    n_last, c_last = n_col[tokens - 1 :, :], c_col[tokens - 1 :, :]
    tail = jnp.where(jnp.abs(n_col - n_last) < 0.5, jnp.exp(jnp.minimum(c_last - c_col, 0.0)), 0.0) * k
    moved = mm_tn(total, tail)
    eye = (row_id == col_id)[:HD, :HD]
    ab_send[h, 0] = (jnp.where(eye, reach[tokens - 1 :, :], 0.0) - moved[HD:]).astype(BF16)
    ab_send[h, 1] = moved[:HD].astype(BF16)
    seen = mm(mm_nt(q.astype(BF16), kb) * ratios, total)
    oloc[:, col] = seen[:, :HD]
    qeff[:, col] = (reach * q - seen[:, HD:]).astype(BF16)


def gather_kernel(
    dq, dk, dv, beta, rows, aq, ak, av,
    kv, qg, sin, oloc, qeff,
    ab_send, ab_recv, t_buf, u_buf, e_buf, s_send,
    own_sem, kv_send, kv_recv, q_send, q_recv, up_send, up_recv, down_send, down_recv,
    c_send, c_recv,
):
    y, z, x = place()
    r, g = (z % 2) * 2 + x, z // 2
    tokens = dq.shape[0]
    across = z + 1 - 2 * (z % 2)
    beyond = z - 1 + 2 * (z % 2)
    peers = [at(y + d, z, x) for d in (1, 2, 3)]
    peers += [at(y + d, z, x + 1) for d in range(4)]
    peers += [at(y, across, x), at(y, across, x + 1), at(y, beyond, x)]
    peers += [at(y, z + d, x) for d in (2, 4, 6)]
    barrier = pltpu.get_barrier_semaphore()
    for peer in peers:
        pl.semaphore_signal(barrier, inc=1, device_id=peer, device_id_type=MESH)
    pl.semaphore_wait(barrier, len(peers))
    sent = []

    def head_cols(h):
        return pl.ds(pl.multiple_of((h % NY) * HD, HD), HD)

    own_k = pltpu.make_async_copy(ak.at[:, head_cols(y)], kv.at[y, z, 0], own_sem.at[0])
    own_v = pltpu.make_async_copy(av.at[:, head_cols(y)], kv.at[y, z, 1], own_sem.at[1])
    own_q = pltpu.make_async_copy(aq.at[:, head_cols(y)], qg.at[y, x], own_sem.at[2])
    own_k.start()
    own_v.start()
    for j in (1, 2, 3):
        to = y - Y_ORDER[j] + NY
        for part, source in enumerate((ak, av)):
            copy = remote(
                source.at[:, head_cols(to)], kv.at[y, z, part],
                kv_send.at[j, part], kv_recv.at[j, part], at(to, z, x),
            )
            copy.start()
            sent.append(copy)

    def piece(j, zz):
        return kv.at[(y + Y_ORDER[j]) % NY, zz % NZ]

    def up(j, hop):
        block = piece(j, z - hop + NZ)
        copy = remote(block, block, up_send.at[j, hop], up_recv.at[j, hop], at(y, z + 1, x))
        copy.start()
        sent.append(copy)

    def down(j, hop):
        block = piece(j, z + hop)
        copy = remote(block, block, down_send.at[j, hop], down_recv.at[j, hop], at(y, z - 1 + NZ, x))
        copy.start()
        sent.append(copy)

    def up_arrived(j, hop):
        block = piece(j, z - hop + NZ)
        remote(block, block, up_send.at[j, hop - 1], up_recv.at[j, hop - 1], at(y, z + 1, x)).wait_recv()

    def down_arrived(j, hop):
        block = piece(j, z + hop)
        remote(block, block, down_send.at[j, hop - 1], down_recv.at[j, hop - 1], at(y, z + 1, x)).wait_recv()

    own_k.wait()
    own_v.wait()
    up(0, 0)
    down(0, 0)
    own_q.start()
    for d in range(4):
        for dx in range(2):
            if d or dx:
                to = y + d
                copy = remote(
                    aq.at[:, head_cols(to)], qg.at[y, x],
                    q_send.at[d, dx], q_recv.at[(NY - d) % NY, dx], at(to, z, x + dx),
                )
                copy.start()
                sent.append(copy)

    low = (
        lax.broadcasted_iota(jnp.int32, (tokens, tokens), 0)
        >= lax.broadcasted_iota(jnp.int32, (tokens, tokens), 1)
    ).astype(F32)
    cum_col = mm_nt(low, rows[...], HIGHEST)
    cum_row = mm_nt(rows[...], low, HIGHEST)

    def first_round(j):
        for part in range(2):
            block = kv.at[(y + Y_ORDER[j]) % NY, z, part]
            remote(block, block, kv_send.at[j, part], kv_recv.at[j, part], at(y + 1, z, x)).wait_recv()
        up(j, 0)
        down(j, 0)

    def later_round(j, hop):
        if hop <= UP_HOPS[j]:
            up_arrived(j, hop)
            if hop < UP_HOPS[j]:
                up(j, hop)
        if hop <= DOWN_HOPS[j]:
            down_arrived(j, hop)
            if hop < DOWN_HOPS[j]:
                down(j, hop)

    for h in range(HEADS):
        delta_head(h, dq, dk, dv, beta, cum_col, cum_row, low, oloc, qeff, ab_send)
        if h:
            first_round(h)

    def of_group(index):
        return at(y, g * 2 + (index % GROUP) // 2, (index % GROUP) % 2)

    def pairs_out():
        for d in (1, 2, 3):
            to = (r + d) % GROUP
            copy = remote(ab_send.at[to], ab_recv.at[r], c_send.at[0, d], c_recv.at[0, d], of_group(to))
            copy.start()
            sent.append(copy)
        ab_recv[r] = ab_send[r]

    def pairs_in():
        for d in (1, 2, 3):
            block = ab_recv.at[(r - d + GROUP) % GROUP]
            remote(block, block, c_send.at[0, d], c_recv.at[0, d], of_group(r + 1)).wait_recv()

    def exchange_out(level, buf, mine, device):
        for d in (1, 2, 3):
            copy = remote(buf.at[mine], buf.at[mine], c_send.at[level, d], c_recv.at[level, d], device(d))
            copy.start()
            sent.append(copy)

    def exchange_in(level, buf, mine, device):
        for d in (1, 2, 3):
            block = buf.at[(mine - d + GROUP) % GROUP]
            remote(block, block, c_send.at[level, d], c_recv.at[level, d], device(d)).wait_recv()

    def fold(buf):
        before = []
        a, b = buf[0, 0].astype(F32), buf[0, 1].astype(F32)
        for i in range(1, GROUP):
            before.append((a, b))
            both = mm(jnp.concatenate([a, b], axis=0), buf[i, 0])
            a, b = both[:HD], both[HD:] + buf[i, 1].astype(F32)
        return before, (a, b)

    in_chain = lambda d: at(y, z + 2 * d, x)
    in_column = lambda d: at(y + d, z, x)

    def level_one():
        pairs_in()
        before, (a, b) = fold(ab_recv)
        for i, (ea, eb) in enumerate(before):
            e_buf[i, 0] = ea
            e_buf[i, 1] = eb
        t_buf[g, 0] = a.astype(BF16)
        t_buf[g, 1] = b.astype(BF16)
        exchange_out(1, t_buf, g, in_chain)

    def level_two():
        exchange_in(1, t_buf, g, in_chain)
        before, (a, b) = fold(t_buf)
        eye = (
            lax.broadcasted_iota(jnp.int32, (HD, HD), 0) == lax.broadcasted_iota(jnp.int32, (HD, HD), 1)
        ).astype(F32)
        fa, fb = eye, jnp.zeros((HD, HD), F32)
        for i, (ea, eb) in enumerate(before):
            fa = jnp.where(g == i + 1, ea, fa)
            fb = jnp.where(g == i + 1, eb, fb)
        e_buf[3, 0] = fa
        e_buf[3, 1] = fb
        u_buf[y, 0] = a.astype(BF16)
        u_buf[y, 1] = b.astype(BF16)
        exchange_out(2, u_buf, y, in_column)

    def level_three():
        exchange_in(2, u_buf, y, in_column)
        state = jnp.zeros((HD, HD), F32)
        b = u_buf[0, 1].astype(F32)
        for i in range(1, NY):
            state = jnp.where(y == i, b, state)
            if i < NY - 1:
                b = mm(b, u_buf[i, 0]) + u_buf[i, 1].astype(F32)
        state = mm(state, e_buf[3, 0]) + e_buf[3, 1]
        s_send[0] = state.astype(BF16)
        for i in range(3):
            s_send[i + 1] = (mm(state, e_buf[i, 0]) + e_buf[i, 1]).astype(BF16)
        for d in (1, 2, 3):
            to = (r + d) % GROUP
            copy = remote(s_send.at[to], sin.at[r], c_send.at[3, d], c_recv.at[3, d], of_group(to))
            copy.start()
            sent.append(copy)
        sin[r] = s_send[r]

    def states_in():
        for d in (1, 2, 3):
            block = sin.at[(r - d + GROUP) % GROUP]
            remote(block, block, c_send.at[3, d], c_recv.at[3, d], of_group(r + 1)).wait_recv()

    pairs_out()
    steps = [(j, hop) for hop in (1, 2, 3, 4) for j in range(4)]
    stages = {2: level_one, 5: level_two, 8: level_three}
    for n, (j, hop) in enumerate(steps):
        if n in stages:
            stages[n]()
        later_round(j, hop)
    states_in()
    own_q.wait()
    for d in range(4):
        for dx in range(2):
            if d or dx:
                block = qg.at[(y + d) % NY, (x + dx) % NX]
                remote(block, block, q_send.at[d, dx], q_recv.at[d, dx], at(y + d, z, x + dx)).wait_recv()
    for copy in sent:
        copy.wait_send()


def attend_kernel(kv, q, o, lse, m_ref, l_ref, acc_ref):
    y, z, x = place()
    tokens = kv.shape[3]
    wide = 2 * tokens
    keys = 2 * tokens
    factor = SCALE * LOG2E

    def block(yy, zp, queries, masked):
        k = jnp.concatenate([kv[yy, 2 * zp, 0], kv[yy, 2 * zp + 1, 0]], axis=0)
        v = jnp.concatenate([kv[yy, 2 * zp, 1], kv[yy, 2 * zp + 1, 1]], axis=0)
        s = mm_nt(k, queries)
        if masked:
            row = lax.broadcasted_iota(jnp.int32, (keys, wide), 0)
            col = lax.broadcasted_iota(jnp.int32, (keys, wide), 1)
            key_at = zp * (4 * tokens) + x * tokens + row + jnp.where(row >= tokens, tokens, 0)
            seen = key_at <= z * wide + col
            s = jnp.where(seen, s, NEG)
        old = m_ref[...]
        new = jnp.maximum(old, jnp.max(s, axis=0, keepdims=True))
        p = jnp.exp2((s - new) * factor)
        if masked:
            p = jnp.where(seen, p, 0.0)
        shrink = jnp.exp2((old - new) * factor)
        l_ref[...] = l_ref[...] * shrink + jnp.sum(p, axis=0, keepdims=True)
        acc_ref[...] = acc_ref[...] * shrink + mm_tn(v, p)
        m_ref[...] = new

    for yq in range(NY):
        queries = jnp.concatenate([q[yq, 0], q[yq, 1]], axis=0)
        m_ref[...] = jnp.full_like(m_ref, NEG)
        l_ref[...] = jnp.zeros_like(l_ref)
        acc_ref[...] = jnp.zeros_like(acc_ref)

        @pl.loop(0, yq * (NZ // 2))
        def _(n):
            block(n // (NZ // 2), n % (NZ // 2), queries, False)

        @pl.loop(0, z // 2)
        def _(n):
            block(yq, n, queries, False)

        block(yq, z // 2, queries, True)
        total = l_ref[...]
        some = total > 0.0
        safe = jnp.where(some, total, 1.0)
        out = acc_ref[...] / safe
        o[yq] = out.T.astype(BF16)
        level = jnp.where(some, m_ref[...] * factor + jnp.log2(safe), NEG)
        lse[yq] = jnp.broadcast_to(level, (8, wide))


def finish_kernel(
    o, lse, hidden, weight, oloc, qeff, sin, dgain, again,
    out,
    o_recv, lse_recv, part, part_recv,
    o_send_sem, o_recv_sem, l_send_sem, l_recv_sem, w_send_sem, w_recv_sem,
):
    y, z, x = place()
    me = lax.axis_index("head")
    tokens, cols = hidden.shape
    others = [(d, dx) for d in range(4) for dx in range(2) if d or dx]
    barrier = pltpu.get_barrier_semaphore()
    for d, dx in others:
        pl.semaphore_signal(barrier, inc=1, device_id=at(y + d, z, x + dx), device_id_type=MESH)
    for d in (1, 2, 3):
        pl.semaphore_signal(barrier, inc=1, device_id={"head": (me + d) % 4}, device_id_type=MESH)
    pl.semaphore_wait(barrier, len(others) + 3)
    sent = []
    for d, dx in others:
        ty, tx = (y + d) % NY, (x + dx) % NX
        rows = pl.ds(pl.multiple_of(tx * tokens, 64), tokens)
        copy = remote(
            o.at[ty, rows], o_recv.at[y, x],
            o_send_sem.at[d, dx], o_recv_sem.at[(NY - d) % NY, dx], at(ty, z, tx),
        )
        copy.start()
        sent.append(copy)
        copy = remote(
            lse.at[ty], lse_recv.at[y, x],
            l_send_sem.at[d, dx], l_recv_sem.at[(NY - d) % NY, dx], at(ty, z, tx),
        )
        copy.start()
        sent.append(copy)
    o_recv[y, x] = o[y, pl.ds(pl.multiple_of(x * tokens, 64), tokens), :]
    lse_recv[y, x] = lse[y]

    delta = []
    for h in range(HEADS):
        col = slice(h * HD, (h + 1) * HD)
        raw = mm_nt(qeff[:, col], sin[h]) + oloc[:, col]
        scaled = raw * lax.rsqrt(jnp.mean(raw * raw, axis=-1, keepdims=True) + EPSILON)
        delta.append(scaled * dgain[...])

    for d, dx in others:
        block = o_recv.at[(y + d) % NY, (x + dx) % NX]
        remote(block, block, o_send_sem.at[d, dx], o_recv_sem.at[d, dx], at(y + d, z, x + dx)).wait_recv()
        block = lse_recv.at[(y + d) % NY, (x + dx) % NX]
        remote(block, block, l_send_sem.at[d, dx], l_recv_sem.at[d, dx], at(y + d, z, x + dx)).wait_recv()

    shares = []
    for h in range(HEADS):
        a, b = lse_recv[h, 0][:1], lse_recv[h, 1][:1]
        top = jnp.maximum(a, b)
        a, b = jnp.exp2(a - top), jnp.exp2(b - top)
        both = a + b
        shares += [a / both, b / both]
    shares = jnp.concatenate(shares, axis=0)
    pick = (
        lax.broadcasted_iota(jnp.int32, (tokens, 2 * tokens), 1)
        == lax.broadcasted_iota(jnp.int32, (tokens, 2 * tokens), 0) + x * tokens
    ).astype(F32)
    shares = mm_nt(pick, shares, HIGHEST)
    combined = []
    for h in range(HEADS):
        raw = (
            o_recv[h, 0].astype(F32) * shares[:, 2 * h : 2 * h + 1]
            + o_recv[h, 1].astype(F32) * shares[:, 2 * h + 1 : 2 * h + 2]
        )
        scaled = raw * lax.rsqrt(jnp.mean(raw * raw, axis=-1, keepdims=True) + EPSILON)
        combined.append((0.5 * (delta[h] + scaled * again[...])).astype(BF16))
    combined = jnp.concatenate(combined, axis=1)
    for d in (1, 2, 3):
        to = (me + d) % 4
        columns = pl.ds(pl.multiple_of(to * cols, HD), cols)
        part[d] = jnp.dot(combined, weight[:, columns], preferred_element_type=F32).astype(BF16)
        copy = remote(part.at[d], part_recv.at[d], w_send_sem.at[d], w_recv_sem.at[d], {"head": to})
        copy.start()
        sent.append(copy)
    total = jnp.dot(
        combined, weight[:, pl.ds(pl.multiple_of(me * cols, HD), cols)], preferred_element_type=F32
    )
    for d in (1, 2, 3):
        block = part_recv.at[d]
        remote(block, block, w_send_sem.at[d], w_recv_sem.at[d], {"head": (me + d) % 4}).wait_recv()
        total = total + part_recv[d].astype(F32)
    out[...] = (hidden[...].astype(F32) + total).astype(BF16)
    for copy in sent:
        copy.wait_send()


VMEM = pl.BlockSpec(memory_space=pltpu.VMEM)
ANY = pl.BlockSpec(memory_space=pl.ANY)
DMA = pltpu.SemaphoreType.DMA
LIMIT = 48 * 1024 * 1024


def local(
    hidden_in, delta_q, delta_k, delta_v, beta, log_decay, resets,
    attn_q, attn_k, attn_v, delta_gain, attn_gain, out_weight,
):
    tokens, cols = delta_q.shape
    struct = jax.ShapeDtypeStruct
    rows = jnp.concatenate(
        [log_decay.T, resets.astype(F32)[None], jnp.zeros((3, tokens), F32)], axis=0
    )
    kv, qg, sin, oloc, qeff = pl.pallas_call(
        gather_kernel,
        out_shape=(
            struct((NY, NZ, 2, tokens, HD), BF16),
            struct((NY, NX, tokens, HD), BF16),
            struct((HEADS, HD, HD), BF16),
            struct((tokens, cols), F32),
            struct((tokens, cols), BF16),
        ),
        in_specs=[VMEM] * 8,
        out_specs=(ANY, ANY, VMEM, VMEM, VMEM),
        scratch_shapes=[
            pltpu.VMEM((HEADS, 2, HD, HD), BF16),
            pltpu.VMEM((GROUP, 2, HD, HD), BF16),
            pltpu.VMEM((GROUP, 2, HD, HD), BF16),
            pltpu.VMEM((NY, 2, HD, HD), BF16),
            pltpu.VMEM((4, 2, HD, HD), F32),
            pltpu.VMEM((GROUP, HD, HD), BF16),
            DMA((3,)),
            DMA((4, 2)), DMA((4, 2)),
            DMA((4, 2)), DMA((4, 2)),
            DMA((4, 4)), DMA((4, 4)),
            DMA((4, 4)), DMA((4, 4)),
            DMA((4, 4)), DMA((4, 4)),
        ],
        compiler_params=pltpu.CompilerParams(
            collective_id=0, has_side_effects=True, vmem_limit_bytes=LIMIT
        ),
    )(delta_q, delta_k, delta_v, beta, rows, attn_q, attn_k, attn_v)
    o, lse = pl.pallas_call(
        attend_kernel,
        out_shape=(struct((NY, NX * tokens, HD), BF16), struct((NY, 8, NX * tokens), F32)),
        in_specs=[VMEM] * 2,
        out_specs=(VMEM, VMEM),
        scratch_shapes=[
            pltpu.VMEM((1, NX * tokens), F32),
            pltpu.VMEM((1, NX * tokens), F32),
            pltpu.VMEM((HD, NX * tokens), F32),
        ],
        compiler_params=pltpu.CompilerParams(vmem_limit_bytes=LIMIT),
    )(kv, qg)
    return pl.pallas_call(
        finish_kernel,
        out_shape=struct((tokens, cols), BF16),
        in_specs=[VMEM] * 9,
        out_specs=VMEM,
        scratch_shapes=[
            pltpu.VMEM((NY, NX, tokens, HD), BF16),
            pltpu.VMEM((NY, NX, 8, NX * tokens), F32),
            pltpu.VMEM((4, tokens, cols), BF16),
            pltpu.VMEM((4, tokens, cols), BF16),
            DMA((4, 2)), DMA((4, 2)),
            DMA((4, 2)), DMA((4, 2)),
            DMA((4,)), DMA((4,)),
        ],
        compiler_params=pltpu.CompilerParams(
            collective_id=1, has_side_effects=True, vmem_limit_bytes=LIMIT
        ),
    )(
        o, lse, hidden_in, out_weight, oloc, qeff, sin,
        delta_gain.reshape(1, HD), attn_gain.reshape(1, HD),
    )


def solution(mesh):
    by_head = P("seq", "head")
    placed = (by_head,) * 6 + (P("seq"),) + (by_head,) * 3 + (P(), P(), P("head", None))
    return jax.shard_map(local, mesh=mesh, in_specs=placed, out_specs=by_head, check_vma=False)
```

```python
import jax
import jax.numpy as jnp
from jax import lax
from jax.experimental import pallas as pl
from jax.experimental.pallas import tpu as pltpu
from jax.sharding import PartitionSpec as P

HD = 128
EPSILON = 1e-06
NY, NZ, NX = 4, 8, 2
HEADS = 4
GROUP = 4
SUB = 64
MESH = pl.DeviceIdType.MESH
HIGHEST = lax.Precision.HIGHEST
F32 = jnp.float32
BF16 = jnp.bfloat16
NEG = -1e30
SCALE = HD**-0.5
LOG2E = 1.4426950408889634
Y_ORDER = (0, 1, 3, 2)
UP_HOPS = (4, 4, 3, 3)
DOWN_HOPS = (3, 3, 4, 4)


def mm(a, b):
    return jnp.dot(a.astype(BF16), b.astype(BF16), preferred_element_type=F32)


def mm_nt(a, b, precision=None):
    return lax.dot_general(
        a, b, (((1,), (1,)), ((), ())), precision=precision, preferred_element_type=F32
    )


def mm_tn(a, b):
    return lax.dot_general(
        a.astype(BF16), b.astype(BF16), (((0,), (0,)), ((), ())), preferred_element_type=F32
    )


def place():
    s = lax.axis_index("seq")
    return s // (NZ * NX), (s // NX) % NZ, s % NX


def at(y, z, x):
    return {"seq": ((y % NY) * NZ + z % NZ) * NX + x % NX}


def remote(src, dst, send, recv, device):
    return pltpu.make_async_remote_copy(
        src_ref=src,
        dst_ref=dst,
        send_sem=send,
        recv_sem=recv,
        device_id=device,
        device_id_type=MESH,
    )


def delta_head(h, dq, dk, dv, betas, cum_col, cum_row, oloc, qeff, ab_send):
    tokens = dq.shape[0]
    col = slice(h * HD, (h + 1) * HD)
    q = dq[:, col].astype(F32)
    k = dk[:, col].astype(F32)
    v = dv[:, col].astype(F32)
    q = q * (lax.rsqrt(jnp.sum(q * q, axis=-1, keepdims=True) + EPSILON) * SCALE)
    k = k * lax.rsqrt(jnp.sum(k * k, axis=-1, keepdims=True) + EPSILON)
    strength = betas[:, h + 8 : h + 9]
    row_id = lax.broadcasted_iota(jnp.int32, (tokens, tokens), 0)
    col_id = lax.broadcasted_iota(jnp.int32, (tokens, tokens), 1)
    c_col, n_col = cum_col[:, h : h + 1], cum_col[:, HEADS : HEADS + 1]
    c_row, n_row = cum_row[h : h + 1, :], cum_row[HEADS : HEADS + 1, :]
    reach = jnp.where(n_col < 0.5, jnp.exp(c_col), 0.0)
    same = (jnp.abs(n_col - n_row) < 0.5) & (row_id >= col_id)
    ratios = jnp.where(same, jnp.exp(jnp.minimum(c_col - c_row, 0.0)), 0.0)
    kb = k.astype(BF16)
    inner = mm_nt(kb, kb)
    system = jnp.where(row_id > col_id, strength * ratios * inner, 0.0)
    near = (row_id // SUB) == (col_id // SUB)
    power = jnp.where(near, -system, 0.0)
    far = jnp.where(near, 0.0, system)
    inverse = jnp.where(row_id == col_id, 1.0, power)
    reached = 2
    while reached < SUB:
        power = mm(power, power)
        inverse = inverse + mm(inverse, power)
        reached *= 2
    right = jnp.concatenate([strength * v, (strength * reach) * k], axis=1)
    solved = mm(inverse, right)
    spread = mm(inverse, far)
    total = solved
    for _ in range((tokens + SUB - 1) // SUB - 1):
        total = solved - mm(spread, total)
    n_last, c_last = n_col[tokens - 1 :, :], c_col[tokens - 1 :, :]
    tail = jnp.where(jnp.abs(n_col - n_last) < 0.5, jnp.exp(jnp.minimum(c_last - c_col, 0.0)), 0.0) * k
    moved = mm_tn(total, tail)
    eye = (row_id == col_id)[:HD, :HD]
    ab_send[h, 0] = (jnp.where(eye, reach[tokens - 1 :, :], 0.0) - moved[HD:]).astype(BF16)
    ab_send[h, 1] = moved[:HD].astype(BF16)
    seen = mm(mm_nt(q.astype(BF16), kb) * ratios, total)
    oloc[:, col] = seen[:, :HD]
    qeff[:, col] = (reach * q - seen[:, HD:]).astype(BF16)


def attend(tiles, k, v, q, m_ref, l_ref, acc_ref, seen=None):
    factor = SCALE * LOG2E
    scores = [mm_nt(k, q[t]) for t in tiles]
    for t, s in zip(tiles, scores):
        if seen is not None:
            s = jnp.where(seen, s, NEG)
        old = m_ref[t]
        new = jnp.maximum(old, jnp.max(s, axis=0, keepdims=True))
        p = jnp.exp2((s - new) * factor)
        if seen is not None:
            p = jnp.where(seen, p, 0.0)
        shrink = jnp.exp2((old - new) * factor)
        l_ref[t] = l_ref[t] * shrink + jnp.sum(p, axis=0, keepdims=True)
        acc_ref[t] = acc_ref[t] * shrink + mm_tn(v, p)
        m_ref[t] = new


def main_kernel(
    dq_in, dk_in, dv_in, beta_in, decay_in, resets_in, aq, ak, av,
    o, lse, sin, oloc, qeff,
    dq, dk, dv, beta, decay, resets, rows,
    kv, qg, m_ref, l_ref, acc_ref,
    ab_send, ab_recv, t_buf, u_buf, e_buf, s_send,
    in_sem, own_sem, kv_send, kv_recv, q_send, q_recv, up_send, up_recv, down_send, down_recv,
    c_send, c_recv,
):
    y, z, x = place()
    r, g = (z % 2) * 2 + x, z // 2
    tokens = dq.shape[0]
    wide = NX * tokens
    loads = [
        pltpu.make_async_copy(a, b, in_sem.at[i])
        for i, (a, b) in enumerate(
            zip((dq_in, dk_in, dv_in, beta_in, decay_in, resets_in), (dq, dk, dv, beta, decay, resets))
        )
    ]
    for load in loads:
        load.start()
    across = z + 1 - 2 * (z % 2)
    beyond = z - 1 + 2 * (z % 2)
    peers = [at(y + d, z, x) for d in (1, 2, 3)]
    peers += [at(y + d, z, x + 1) for d in range(4)]
    peers += [at(y, across, x), at(y, across, x + 1), at(y, beyond, x)]
    peers += [at(y, z + d, x) for d in (2, 4, 6)]
    barrier = pltpu.get_barrier_semaphore()
    for peer in peers:
        pl.semaphore_signal(barrier, inc=1, device_id=peer, device_id_type=MESH)
    pl.semaphore_wait(barrier, len(peers))
    sent = []

    def head_cols(h):
        return pl.ds(pl.multiple_of((h % NY) * HD, HD), HD)

    def q_rows(xx):
        return pl.ds(pl.multiple_of((xx % NX) * tokens, 64), tokens)

    own_k = pltpu.make_async_copy(ak.at[:, head_cols(y)], kv.at[y, z, 0], own_sem.at[0])
    own_v = pltpu.make_async_copy(av.at[:, head_cols(y)], kv.at[y, z, 1], own_sem.at[1])
    own_q = pltpu.make_async_copy(aq.at[:, head_cols(y)], qg.at[y, q_rows(x)], own_sem.at[2])
    own_k.start()
    own_v.start()
    for j in (1, 2, 3):
        to = y - Y_ORDER[j] + NY
        for part, source in enumerate((ak, av)):
            copy = remote(
                source.at[:, head_cols(to)], kv.at[y, z, part],
                kv_send.at[j, part], kv_recv.at[j, part], at(to, z, x),
            )
            copy.start()
            sent.append(copy)

    def y_of(j):
        step = Y_ORDER[j] if isinstance(j, int) else j + jnp.where(j == 2, 1, 0) - jnp.where(j == 3, 1, 0)
        return (y + step) % NY

    def upward(j, hop):
        block = kv.at[y_of(j), (z - hop + NZ) % NZ]
        return remote(block, block, up_send.at[j, hop], up_recv.at[j, hop], at(y, z + 1, x))

    def downward(j, hop):
        block = kv.at[y_of(j), (z + hop) % NZ]
        return remote(block, block, down_send.at[j, hop], down_recv.at[j, hop], at(y, z - 1 + NZ, x))

    def arrive_up(j, hop):
        block = kv.at[y_of(j), (z - hop + NZ) % NZ]
        remote(block, block, up_send.at[j, hop - 1], up_recv.at[j, hop - 1], at(y, z + 1, x)).wait_recv()

    def arrive_down(j, hop):
        block = kv.at[y_of(j), (z + hop) % NZ]
        remote(block, block, down_send.at[j, hop - 1], down_recv.at[j, hop - 1], at(y, z + 1, x)).wait_recv()

    own_k.wait()
    own_v.wait()
    upward(0, 0).start()
    downward(0, 0).start()
    own_q.start()
    for d in range(4):
        for dx in range(2):
            if d or dx:
                to = y + d
                copy = remote(
                    aq.at[:, head_cols(to)], qg.at[y, q_rows(x)],
                    q_send.at[d, dx], q_recv.at[(NY - d) % NY, dx], at(to, z, x + dx),
                )
                copy.start()
                sent.append(copy)

    for load in loads:
        load.wait()
    rows[...] = jnp.zeros_like(rows)
    rows[0:HEADS] = decay[...]
    rows[HEADS : HEADS + 1] = resets[...].astype(F32)
    rows[8 : 8 + HEADS] = beta[...]
    row_id = lax.broadcasted_iota(jnp.int32, (tokens, tokens), 0)
    col_id = lax.broadcasted_iota(jnp.int32, (tokens, tokens), 1)
    low = (row_id >= col_id).astype(F32)
    cum_col = mm_nt(low, rows[...], HIGHEST)
    cum_row = mm_nt(rows[...], low, HIGHEST)
    betas = mm_nt((row_id == col_id).astype(F32), rows[...], HIGHEST)

    def first_round(j):
        for part in range(2):
            block = kv.at[y_of(j), z, part]
            remote(block, block, kv_send.at[j, part], kv_recv.at[j, part], at(y + 1, z, x)).wait_recv()
        upward(j, 0).start()
        downward(j, 0).start()

    def forward_both(j, hop):
        arrive_up(j, hop)
        upward(j, hop).start()
        arrive_down(j, hop)
        downward(j, hop).start()

    for h in range(HEADS):
        delta_head(h, dq, dk, dv, betas, cum_col, cum_row, oloc, qeff, ab_send)
        if h:
            first_round(h)
        if h >= 2:
            forward_both(h - 2, 1)

    def of_group(index):
        return at(y, g * 2 + (index % GROUP) // 2, (index % GROUP) % 2)

    def pairs_out():
        for d in (1, 2, 3):
            to = (r + d) % GROUP
            copy = remote(ab_send.at[to], ab_recv.at[r], c_send.at[0, d], c_recv.at[0, d], of_group(to))
            copy.start()
            sent.append(copy)
        ab_recv[r] = ab_send[r]

    def pairs_in():
        for d in (1, 2, 3):
            block = ab_recv.at[(r - d + GROUP) % GROUP]
            remote(block, block, c_send.at[0, d], c_recv.at[0, d], of_group(r + 1)).wait_recv()

    def exchange(level, buf, mine, device):
        return [
            remote(buf.at[mine], buf.at[mine], c_send.at[level, d], c_recv.at[level, d], device(d))
            for d in (1, 2, 3)
        ]

    def exchange_in(level, buf, mine, device):
        for d in (1, 2, 3):
            block = buf.at[(mine - d + GROUP) % GROUP]
            remote(block, block, c_send.at[level, d], c_recv.at[level, d], device(d)).wait_recv()

    def fold(buf):
        before = []
        a, b = buf[0, 0].astype(F32), buf[0, 1].astype(F32)
        for i in range(1, GROUP):
            before.append((a, b))
            both = mm(jnp.concatenate([a, b], axis=0), buf[i, 0])
            a, b = both[:HD], both[HD:] + buf[i, 1].astype(F32)
        return before, (a, b)

    in_chain = lambda d: at(y, z + 2 * d, x)
    in_column = lambda d: at(y + d, z, x)

    def level_one():
        pairs_in()
        before, (a, b) = fold(ab_recv)
        for i, (ea, eb) in enumerate(before):
            e_buf[i, 0] = ea
            e_buf[i, 1] = eb
        t_buf[g, 0] = a.astype(BF16)
        t_buf[g, 1] = b.astype(BF16)
        for copy in exchange(1, t_buf, g, in_chain):
            copy.start()

    def level_two():
        exchange_in(1, t_buf, g, in_chain)
        before, (a, b) = fold(t_buf)
        eye = (row_id == col_id)[:HD, :HD].astype(F32)
        fa, fb = eye, jnp.zeros((HD, HD), F32)
        for i, (ea, eb) in enumerate(before):
            fa = jnp.where(g == i + 1, ea, fa)
            fb = jnp.where(g == i + 1, eb, fb)
        e_buf[3, 0] = fa
        e_buf[3, 1] = fb
        u_buf[y, 0] = a.astype(BF16)
        u_buf[y, 1] = b.astype(BF16)
        for copy in exchange(2, u_buf, y, in_column):
            copy.start()

    def states_out():
        copies = []
        for d in (1, 2, 3):
            to = (r + d) % GROUP
            copies.append(remote(s_send.at[to], sin.at[r], c_send.at[3, d], c_recv.at[3, d], of_group(to)))
        return copies

    def level_three():
        exchange_in(2, u_buf, y, in_column)
        state = jnp.zeros((HD, HD), F32)
        b = u_buf[0, 1].astype(F32)
        for i in range(1, NY):
            state = jnp.where(y == i, b, state)
            if i < NY - 1:
                b = mm(b, u_buf[i, 0]) + u_buf[i, 1].astype(F32)
        state = mm(state, e_buf[3, 0]) + e_buf[3, 1]
        s_send[0] = state.astype(BF16)
        for i in range(3):
            s_send[i + 1] = (mm(state, e_buf[i, 0]) + e_buf[i, 1]).astype(BF16)
        for copy in states_out():
            copy.start()
        sin[r] = s_send[r]

    def states_in():
        for d in (1, 2, 3):
            block = sin.at[(r - d + GROUP) % GROUP]
            remote(block, block, c_send.at[3, d], c_recv.at[3, d], of_group(r + 1)).wait_recv()

    pairs_out()
    forward_both(2, 1)
    forward_both(3, 1)

    m_ref[...] = jnp.full_like(m_ref, NEG)
    l_ref[...] = jnp.zeros_like(l_ref)
    acc_ref[...] = jnp.zeros_like(acc_ref)
    own_q.wait()
    for d in range(4):
        for dx in range(2):
            if d or dx:
                block = qg.at[(y + d) % NY, q_rows(x + dx)]
                remote(block, block, q_send.at[d, dx], q_recv.at[d, dx], at(y + d, z, x + dx)).wait_recv()

    def attend_later(yk, k, v):
        for case in range(NY - 1):

            @pl.when(yk == case)
            def _():
                attend(range(case + 1, NY), k(), v(), qg, m_ref, l_ref, acc_ref)

    def attend_single(yk, zk):
        attend_later(yk, lambda: kv[yk, zk, 0], lambda: kv[yk, zk, 1])

    def attend_same(yk, zk):
        @pl.when(zk < z)
        def _():
            attend([yk], kv[yk, zk, 0], kv[yk, zk, 1], qg, m_ref, l_ref, acc_ref)

    @pl.loop(0, NY)
    def _(j):
        yk = y_of(j)
        attend_single(yk, z)
        key_at = lax.broadcasted_iota(jnp.int32, (tokens, wide), 0) + x * tokens
        seen = key_at <= lax.broadcasted_iota(jnp.int32, (tokens, wide), 1)
        attend([yk], kv[yk, z, 0], kv[yk, z, 1], qg, m_ref, l_ref, acc_ref, seen)

    stages = {0: level_one, 4: level_two, 8: level_three}

    @pl.loop(0, 12)
    def _(n):
        j, hop = n % NY, n // NY + 1
        for when, stage in stages.items():
            pl.when(n == when)(stage)
        yk = y_of(j)
        before, after = (z - hop + NZ) % NZ, (z + hop) % NZ
        attend_later(
            yk,
            lambda: jnp.concatenate([kv[yk, before, 0], kv[yk, after, 0]], axis=0),
            lambda: jnp.concatenate([kv[yk, before, 1], kv[yk, after, 1]], axis=0),
        )
        attend_same(yk, before)
        attend_same(yk, after)

        @pl.when((hop < 3) | (j < 2))
        def _():
            arrive_up(j, hop + 1)

        @pl.when((hop == 1) | ((hop == 2) & (j < 2)))
        def _():
            upward(j, hop + 1).start()

        @pl.when((hop < 3) | (j >= 2))
        def _():
            arrive_down(j, hop + 1)

        @pl.when((hop == 1) | ((hop == 2) & (j >= 2)))
        def _():
            downward(j, hop + 1).start()

    @pl.loop(0, NY)
    def _(j):
        yk = y_of(j)
        attend_single(yk, (z + 4) % NZ)
        attend_same(yk, (z + 4) % NZ)

    for t in range(NY):
        total = l_ref[t]
        some = total > 0.0
        safe = jnp.where(some, total, 1.0)
        o[t] = (acc_ref[t] / safe).T.astype(BF16)
        level = jnp.where(some, m_ref[t] * (SCALE * LOG2E) + jnp.log2(safe), NEG)
        lse[t] = jnp.broadcast_to(level, (8, wide))
    states_in()
    for copy in sent + exchange(1, t_buf, g, in_chain) + exchange(2, u_buf, y, in_column) + states_out():
        copy.wait_send()
    for j in range(NY):
        for hop in range(4):
            if hop < UP_HOPS[j]:
                upward(j, hop).wait_send()
            if hop < DOWN_HOPS[j]:
                downward(j, hop).wait_send()


def finish_kernel(
    o, lse, hidden, weight, oloc, qeff, sin, dgain, again,
    out,
    o_recv, lse_recv, part, part_recv,
    o_send_sem, o_recv_sem, l_send_sem, l_recv_sem, w_send_sem, w_recv_sem,
):
    y, z, x = place()
    me = lax.axis_index("head")
    tokens, cols = hidden.shape
    others = [(d, dx) for d in range(4) for dx in range(2) if d or dx]
    barrier = pltpu.get_barrier_semaphore()
    for d, dx in others:
        pl.semaphore_signal(barrier, inc=1, device_id=at(y + d, z, x + dx), device_id_type=MESH)
    for d in (1, 2, 3):
        pl.semaphore_signal(barrier, inc=1, device_id={"head": (me + d) % 4}, device_id_type=MESH)
    pl.semaphore_wait(barrier, len(others) + 3)
    sent = []
    for d, dx in others:
        ty, tx = (y + d) % NY, (x + dx) % NX
        rows = pl.ds(pl.multiple_of(tx * tokens, 64), tokens)
        copy = remote(
            o.at[ty, rows], o_recv.at[y, x],
            o_send_sem.at[d, dx], o_recv_sem.at[(NY - d) % NY, dx], at(ty, z, tx),
        )
        copy.start()
        sent.append(copy)
        copy = remote(
            lse.at[ty], lse_recv.at[y, x],
            l_send_sem.at[d, dx], l_recv_sem.at[(NY - d) % NY, dx], at(ty, z, tx),
        )
        copy.start()
        sent.append(copy)
    o_recv[y, x] = o[y, pl.ds(pl.multiple_of(x * tokens, 64), tokens), :]
    lse_recv[y, x] = lse[y]

    delta = []
    for h in range(HEADS):
        col = slice(h * HD, (h + 1) * HD)
        raw = mm_nt(qeff[:, col], sin[h]) + oloc[:, col]
        scaled = raw * lax.rsqrt(jnp.mean(raw * raw, axis=-1, keepdims=True) + EPSILON)
        delta.append(scaled * dgain[...])

    for d, dx in others:
        block = o_recv.at[(y + d) % NY, (x + dx) % NX]
        remote(block, block, o_send_sem.at[d, dx], o_recv_sem.at[d, dx], at(y + d, z, x + dx)).wait_recv()
        block = lse_recv.at[(y + d) % NY, (x + dx) % NX]
        remote(block, block, l_send_sem.at[d, dx], l_recv_sem.at[d, dx], at(y + d, z, x + dx)).wait_recv()

    shares = []
    for h in range(HEADS):
        a, b = lse_recv[h, 0][:1], lse_recv[h, 1][:1]
        top = jnp.maximum(a, b)
        a, b = jnp.exp2(a - top), jnp.exp2(b - top)
        both = a + b
        shares += [a / both, b / both]
    shares = jnp.concatenate(shares, axis=0)
    pick = (
        lax.broadcasted_iota(jnp.int32, (tokens, 2 * tokens), 1)
        == lax.broadcasted_iota(jnp.int32, (tokens, 2 * tokens), 0) + x * tokens
    ).astype(F32)
    shares = mm_nt(pick, shares, HIGHEST)
    combined = []
    for h in range(HEADS):
        raw = (
            o_recv[h, 0].astype(F32) * shares[:, 2 * h : 2 * h + 1]
            + o_recv[h, 1].astype(F32) * shares[:, 2 * h + 1 : 2 * h + 2]
        )
        scaled = raw * lax.rsqrt(jnp.mean(raw * raw, axis=-1, keepdims=True) + EPSILON)
        combined.append((0.5 * (delta[h] + scaled * again[...])).astype(BF16))
    combined = jnp.concatenate(combined, axis=1)
    for d in (1, 2, 3):
        to = (me + d) % 4
        columns = pl.ds(pl.multiple_of(to * cols, HD), cols)
        part[d] = jnp.dot(combined, weight[:, columns], preferred_element_type=F32).astype(BF16)
        copy = remote(part.at[d], part_recv.at[d], w_send_sem.at[d], w_recv_sem.at[d], {"head": to})
        copy.start()
        sent.append(copy)
    total = jnp.dot(
        combined, weight[:, pl.ds(pl.multiple_of(me * cols, HD), cols)], preferred_element_type=F32
    )
    for d in (1, 2, 3):
        block = part_recv.at[d]
        remote(block, block, w_send_sem.at[d], w_recv_sem.at[d], {"head": (me + d) % 4}).wait_recv()
        total = total + part_recv[d].astype(F32)
    out[...] = (hidden[...].astype(F32) + total).astype(BF16)
    for copy in sent:
        copy.wait_send()


VMEM = pl.BlockSpec(memory_space=pltpu.VMEM)
ANY = pl.BlockSpec(memory_space=pl.ANY)
DMA = pltpu.SemaphoreType.DMA
LIMIT = 60 * 1024 * 1024


def local(
    hidden_in, delta_q, delta_k, delta_v, beta, log_decay, resets,
    attn_q, attn_k, attn_v, delta_gain, attn_gain, out_weight,
):
    tokens, cols = delta_q.shape
    struct = jax.ShapeDtypeStruct
    wide = NX * tokens
    vmem = pltpu.VMEM
    o, lse, sin, oloc, qeff = pl.pallas_call(
        main_kernel,
        out_shape=(
            struct((NY, wide, HD), BF16),
            struct((NY, 8, wide), F32),
            struct((HEADS, HD, HD), BF16),
            struct((tokens, cols), F32),
            struct((tokens, cols), BF16),
        ),
        in_specs=[ANY] * 9,
        out_specs=(VMEM,) * 5,
        scratch_shapes=[
            vmem((tokens, cols), BF16), vmem((tokens, cols), BF16), vmem((tokens, cols), BF16),
            vmem((HEADS, tokens), F32), vmem((HEADS, tokens), F32), vmem((1, tokens), jnp.int32),
            vmem((16, tokens), F32),
            vmem((NY, NZ, 2, tokens, HD), BF16),
            vmem((NY, wide, HD), BF16),
            vmem((NY, 1, wide), F32),
            vmem((NY, 1, wide), F32),
            vmem((NY, HD, wide), F32),
            vmem((HEADS, 2, HD, HD), BF16),
            vmem((GROUP, 2, HD, HD), BF16),
            vmem((GROUP, 2, HD, HD), BF16),
            vmem((NY, 2, HD, HD), BF16),
            vmem((4, 2, HD, HD), F32),
            vmem((GROUP, HD, HD), BF16),
            DMA((6,)),
            DMA((3,)),
            DMA((4, 2)), DMA((4, 2)),
            DMA((4, 2)), DMA((4, 2)),
            DMA((4, 4)), DMA((4, 4)),
            DMA((4, 4)), DMA((4, 4)),
            DMA((4, 4)), DMA((4, 4)),
        ],
        compiler_params=pltpu.CompilerParams(
            collective_id=0, has_side_effects=True, vmem_limit_bytes=LIMIT
        ),
    )(
        delta_q, delta_k, delta_v, beta.T, log_decay.T, resets.reshape(1, tokens),
        attn_q, attn_k, attn_v,
    )
    return pl.pallas_call(
        finish_kernel,
        out_shape=struct((tokens, cols), BF16),
        in_specs=[VMEM] * 9,
        out_specs=VMEM,
        scratch_shapes=[
            pltpu.VMEM((NY, NX, tokens, HD), BF16),
            pltpu.VMEM((NY, NX, 8, NX * tokens), F32),
            pltpu.VMEM((4, tokens, cols), BF16),
            pltpu.VMEM((4, tokens, cols), BF16),
            DMA((4, 2)), DMA((4, 2)),
            DMA((4, 2)), DMA((4, 2)),
            DMA((4,)), DMA((4,)),
        ],
        compiler_params=pltpu.CompilerParams(
            collective_id=1, has_side_effects=True, vmem_limit_bytes=LIMIT
        ),
    )(
        o, lse, hidden_in, out_weight, oloc, qeff, sin,
        delta_gain.reshape(1, HD), attn_gain.reshape(1, HD),
    )


def solution(mesh):
    by_head = P("seq", "head")
    placed = (by_head,) * 6 + (P("seq"),) + (by_head,) * 3 + (P(), P(), P("head", None))
    return jax.shard_map(local, mesh=mesh, in_specs=placed, out_specs=by_head, check_vma=False)
```

```python
import jax
import jax.numpy as jnp
from jax import lax
from jax.experimental import pallas as pl
from jax.experimental.pallas import tpu as pltpu
from jax.sharding import PartitionSpec as P

HD = 128
EPSILON = 1e-06
NY, NZ, NX = 4, 8, 2
HEADS = 4
GROUP = 4
SUB = 64
MESH = pl.DeviceIdType.MESH
HIGHEST = lax.Precision.HIGHEST
F32 = jnp.float32
BF16 = jnp.bfloat16
NEG = -1e30
SCALE = HD**-0.5
LOG2E = 1.4426950408889634
Y_ORDER = (0, 1, 3, 2)
UP_HOPS = (4, 4, 3, 3)
DOWN_HOPS = (3, 3, 4, 4)


def mm(a, b):
    return jnp.dot(a.astype(BF16), b.astype(BF16), preferred_element_type=F32)


def mm_nt(a, b, precision=None):
    return lax.dot_general(
        a, b, (((1,), (1,)), ((), ())), precision=precision, preferred_element_type=F32
    )


def mm_tn(a, b):
    return lax.dot_general(
        a.astype(BF16), b.astype(BF16), (((0,), (0,)), ((), ())), preferred_element_type=F32
    )


def place():
    s = lax.axis_index("seq")
    return s // (NZ * NX), (s // NX) % NZ, s % NX


def at(y, z, x):
    return {"seq": ((y % NY) * NZ + z % NZ) * NX + x % NX}


def remote(src, dst, send, recv, device):
    return pltpu.make_async_remote_copy(
        src_ref=src,
        dst_ref=dst,
        send_sem=send,
        recv_sem=recv,
        device_id=device,
        device_id_type=MESH,
    )


def delta_head(h, dq, dk, dv, betas, cum_col, cum_row, oloc, qeff, ab_send):
    tokens = dq.shape[0]
    col = slice(h * HD, (h + 1) * HD)
    q = dq[:, col].astype(F32)
    k = dk[:, col].astype(F32)
    v = dv[:, col].astype(F32)
    q = q * (lax.rsqrt(jnp.sum(q * q, axis=-1, keepdims=True) + EPSILON) * SCALE)
    k = k * lax.rsqrt(jnp.sum(k * k, axis=-1, keepdims=True) + EPSILON)
    strength = betas[:, h + 8 : h + 9]
    row_id = lax.broadcasted_iota(jnp.int32, (tokens, tokens), 0)
    col_id = lax.broadcasted_iota(jnp.int32, (tokens, tokens), 1)
    c_col, n_col = cum_col[:, h : h + 1], cum_col[:, HEADS : HEADS + 1]
    c_row, n_row = cum_row[h : h + 1, :], cum_row[HEADS : HEADS + 1, :]
    reach = jnp.where(n_col < 0.5, jnp.exp(c_col), 0.0)
    same = (jnp.abs(n_col - n_row) < 0.5) & (row_id >= col_id)
    ratios = jnp.where(same, jnp.exp(jnp.minimum(c_col - c_row, 0.0)), 0.0)
    kb = k.astype(BF16)
    inner = mm_nt(kb, kb)
    system = jnp.where(row_id > col_id, strength * ratios * inner, 0.0)
    near = (row_id // SUB) == (col_id // SUB)
    power = jnp.where(near, -system, 0.0)
    far = jnp.where(near, 0.0, system)
    inverse = jnp.where(row_id == col_id, 1.0, power)
    reached = 2
    while reached < SUB:
        power = mm(power, power)
        inverse = inverse + mm(inverse, power)
        reached *= 2
    right = jnp.concatenate([strength * v, (strength * reach) * k], axis=1)
    solved = mm(inverse, right)
    spread = mm(inverse, far)
    total = solved
    for _ in range((tokens + SUB - 1) // SUB - 1):
        total = solved - mm(spread, total)
    n_last, c_last = n_col[tokens - 1 :, :], c_col[tokens - 1 :, :]
    tail = jnp.where(jnp.abs(n_col - n_last) < 0.5, jnp.exp(jnp.minimum(c_last - c_col, 0.0)), 0.0) * k
    moved = mm_tn(total, tail)
    eye = (row_id == col_id)[:HD, :HD]
    ab_send[h, 0] = (jnp.where(eye, reach[tokens - 1 :, :], 0.0) - moved[HD:]).astype(BF16)
    ab_send[h, 1] = moved[:HD].astype(BF16)
    seen = mm(mm_nt(q.astype(BF16), kb) * ratios, total)
    oloc[:, col] = seen[:, :HD]
    qeff[:, col] = (reach * q - seen[:, HD:]).astype(BF16)


def attend(tiles, k, v, q, m_ref, l_ref, acc_ref, seen=None):
    factor = SCALE * LOG2E
    scores = [mm_nt(k, q[t]) for t in tiles]
    for t, s in zip(tiles, scores):
        if seen is not None:
            s = jnp.where(seen, s, NEG)
        old = m_ref[t]
        new = jnp.maximum(old, jnp.max(s, axis=0, keepdims=True))
        p = jnp.exp2((s - new) * factor)
        if seen is not None:
            p = jnp.where(seen, p, 0.0)
        shrink = jnp.exp2((old - new) * factor)
        l_ref[t] = l_ref[t] * shrink + jnp.sum(p, axis=0, keepdims=True)
        acc_ref[t] = acc_ref[t] * shrink + mm_tn(v, p)
        m_ref[t] = new


def main_kernel(
    dq_in, dk_in, dv_in, beta_in, decay_in, resets_in, aq, ak, av, weight, dgain_in, again_in,
    out,
    o, lse, sin, oloc, qeff, dgain, again, normed, o_recv, lse_recv, comb, wcol,
    dq, dk, dv, beta, decay, resets, rows,
    kv, qg, m_ref, l_ref, acc_ref,
    ab_send, ab_recv, t_buf, u_buf, e_buf, s_send,
    in_sem, own_sem, kv_send, kv_recv, q_send, q_recv, up_send, up_recv, down_send, down_recv,
    c_send, c_recv,
    o_send_sem, o_recv_sem, l_send_sem, l_recv_sem, w_send, w_recv, ag_send, ag_recv, relay_send, relay_recv,
):
    y, z, x = place()
    me = lax.axis_index("head")
    sibling, facing = me + 1 - 2 * (me % 2), (me + 2) % 4
    diagonal = (sibling + 2) % 4
    cols = dq.shape[1]
    r, g = (z % 2) * 2 + x, z // 2
    tokens = dq.shape[0]
    wide = NX * tokens
    loads = [
        pltpu.make_async_copy(a, b, in_sem.at[i])
        for i, (a, b) in enumerate(
            zip(
                (dq_in, dk_in, dv_in, beta_in, decay_in, resets_in, dgain_in, again_in),
                (dq, dk, dv, beta, decay, resets, dgain, again),
            )
        )
    ]
    for load in loads:
        load.start()
    across = z + 1 - 2 * (z % 2)
    beyond = z - 1 + 2 * (z % 2)
    peers = [at(y + d, z, x) for d in (1, 2, 3)]
    peers += [at(y + d, z, x + 1) for d in range(4)]
    peers += [at(y, across, x), at(y, across, x + 1), at(y, beyond, x)]
    peers += [at(y, z + d, x) for d in (2, 4, 6)]
    peers += [{"head": (me + d) % 4} for d in (1, 2, 3)]
    barrier = pltpu.get_barrier_semaphore()
    for peer in peers:
        pl.semaphore_signal(barrier, inc=1, device_id=peer, device_id_type=MESH)
    pl.semaphore_wait(barrier, len(peers))
    sent = []

    def head_cols(h):
        return pl.ds(pl.multiple_of((h % NY) * HD, HD), HD)

    def q_rows(xx):
        return pl.ds(pl.multiple_of((xx % NX) * tokens, 64), tokens)

    own_k = pltpu.make_async_copy(ak.at[:, head_cols(y)], kv.at[y, z, 0], own_sem.at[0])
    own_v = pltpu.make_async_copy(av.at[:, head_cols(y)], kv.at[y, z, 1], own_sem.at[1])
    own_q = pltpu.make_async_copy(aq.at[:, head_cols(y)], qg.at[y, q_rows(x)], own_sem.at[2])
    own_k.start()
    own_v.start()
    for j in (1, 2, 3):
        to = y - Y_ORDER[j] + NY
        for part, source in enumerate((ak, av)):
            copy = remote(
                source.at[:, head_cols(to)], kv.at[y, z, part],
                kv_send.at[j, part], kv_recv.at[j, part], at(to, z, x),
            )
            copy.start()
            sent.append(copy)

    def y_of(j):
        step = Y_ORDER[j] if isinstance(j, int) else j + jnp.where(j == 2, 1, 0) - jnp.where(j == 3, 1, 0)
        return (y + step) % NY

    def upward(j, hop):
        block = kv.at[y_of(j), (z - hop + NZ) % NZ]
        return remote(block, block, up_send.at[j, hop], up_recv.at[j, hop], at(y, z + 1, x))

    def downward(j, hop):
        block = kv.at[y_of(j), (z + hop) % NZ]
        return remote(block, block, down_send.at[j, hop], down_recv.at[j, hop], at(y, z - 1 + NZ, x))

    def arrive_up(j, hop):
        block = kv.at[y_of(j), (z - hop + NZ) % NZ]
        remote(block, block, up_send.at[j, hop - 1], up_recv.at[j, hop - 1], at(y, z + 1, x)).wait_recv()

    def arrive_down(j, hop):
        block = kv.at[y_of(j), (z + hop) % NZ]
        remote(block, block, down_send.at[j, hop - 1], down_recv.at[j, hop - 1], at(y, z + 1, x)).wait_recv()

    own_k.wait()
    own_v.wait()
    upward(0, 0).start()
    downward(0, 0).start()
    own_q.start()
    for d in range(4):
        for dx in range(2):
            if d or dx:
                to = y + d
                copy = remote(
                    aq.at[:, head_cols(to)], qg.at[y, q_rows(x)],
                    q_send.at[d, dx], q_recv.at[(NY - d) % NY, dx], at(to, z, x + dx),
                )
                copy.start()
                sent.append(copy)

    for load in loads:
        load.wait()
    rows[...] = jnp.zeros_like(rows)
    rows[0:HEADS] = decay[...]
    rows[HEADS : HEADS + 1] = resets[...].astype(F32)
    rows[8 : 8 + HEADS] = beta[...]
    row_id = lax.broadcasted_iota(jnp.int32, (tokens, tokens), 0)
    col_id = lax.broadcasted_iota(jnp.int32, (tokens, tokens), 1)
    low = (row_id >= col_id).astype(F32)
    cum_col = mm_nt(low, rows[...], HIGHEST)
    cum_row = mm_nt(rows[...], low, HIGHEST)
    betas = mm_nt((row_id == col_id).astype(F32), rows[...], HIGHEST)

    def first_round(j):
        for part in range(2):
            block = kv.at[y_of(j), z, part]
            remote(block, block, kv_send.at[j, part], kv_recv.at[j, part], at(y + 1, z, x)).wait_recv()
        upward(j, 0).start()
        downward(j, 0).start()

    def forward_both(j, hop):
        arrive_up(j, hop)
        upward(j, hop).start()
        arrive_down(j, hop)
        downward(j, hop).start()

    for h in range(HEADS):
        delta_head(h, dq, dk, dv, betas, cum_col, cum_row, oloc, qeff, ab_send)
        if h:
            first_round(h)
        if h >= 2:
            forward_both(h - 2, 1)

    def of_group(index):
        return at(y, g * 2 + (index % GROUP) // 2, (index % GROUP) % 2)

    def pairs_out():
        for d in (1, 2, 3):
            to = (r + d) % GROUP
            copy = remote(ab_send.at[to], ab_recv.at[r], c_send.at[0, d], c_recv.at[0, d], of_group(to))
            copy.start()
            sent.append(copy)
        ab_recv[r] = ab_send[r]

    def pairs_in():
        for d in (1, 2, 3):
            block = ab_recv.at[(r - d + GROUP) % GROUP]
            remote(block, block, c_send.at[0, d], c_recv.at[0, d], of_group(r + 1)).wait_recv()

    def exchange(level, buf, mine, device):
        return [
            remote(buf.at[mine], buf.at[mine], c_send.at[level, d], c_recv.at[level, d], device(d))
            for d in (1, 2, 3)
        ]

    def exchange_in(level, buf, mine, device):
        for d in (1, 2, 3):
            block = buf.at[(mine - d + GROUP) % GROUP]
            remote(block, block, c_send.at[level, d], c_recv.at[level, d], device(d)).wait_recv()

    def fold(buf):
        before = []
        a, b = buf[0, 0].astype(F32), buf[0, 1].astype(F32)
        for i in range(1, GROUP):
            before.append((a, b))
            both = mm(jnp.concatenate([a, b], axis=0), buf[i, 0])
            a, b = both[:HD], both[HD:] + buf[i, 1].astype(F32)
        return before, (a, b)

    in_chain = lambda d: at(y, z + 2 * d, x)
    in_column = lambda d: at(y + d, z, x)

    def level_one():
        pairs_in()
        before, (a, b) = fold(ab_recv)
        for i, (ea, eb) in enumerate(before):
            e_buf[i, 0] = ea
            e_buf[i, 1] = eb
        t_buf[g, 0] = a.astype(BF16)
        t_buf[g, 1] = b.astype(BF16)
        for copy in exchange(1, t_buf, g, in_chain):
            copy.start()

    def level_two():
        exchange_in(1, t_buf, g, in_chain)
        before, (a, b) = fold(t_buf)
        eye = (row_id == col_id)[:HD, :HD].astype(F32)
        fa, fb = eye, jnp.zeros((HD, HD), F32)
        for i, (ea, eb) in enumerate(before):
            fa = jnp.where(g == i + 1, ea, fa)
            fb = jnp.where(g == i + 1, eb, fb)
        e_buf[3, 0] = fa
        e_buf[3, 1] = fb
        u_buf[y, 0] = a.astype(BF16)
        u_buf[y, 1] = b.astype(BF16)
        for copy in exchange(2, u_buf, y, in_column):
            copy.start()

    def states_out():
        copies = []
        for d in (1, 2, 3):
            to = (r + d) % GROUP
            copies.append(remote(s_send.at[to], sin.at[r], c_send.at[3, d], c_recv.at[3, d], of_group(to)))
        return copies

    def level_three():
        exchange_in(2, u_buf, y, in_column)
        state = jnp.zeros((HD, HD), F32)
        b = u_buf[0, 1].astype(F32)
        for i in range(1, NY):
            state = jnp.where(y == i, b, state)
            if i < NY - 1:
                b = mm(b, u_buf[i, 0]) + u_buf[i, 1].astype(F32)
        state = mm(state, e_buf[3, 0]) + e_buf[3, 1]
        s_send[0] = state.astype(BF16)
        for i in range(3):
            s_send[i + 1] = (mm(state, e_buf[i, 0]) + e_buf[i, 1]).astype(BF16)
        for copy in states_out():
            copy.start()
        sin[r] = s_send[r]

    def states_in():
        for d in (1, 2, 3):
            block = sin.at[(r - d + GROUP) % GROUP]
            remote(block, block, c_send.at[3, d], c_recv.at[3, d], of_group(r + 1)).wait_recv()

    def weight_cols(device):
        return weight.at[:, pl.ds(pl.multiple_of(device * cols, HD), cols)]

    def weights_out():
        own_w.start()
        for d in (1, 2, 3):
            to = (me + d) % 4
            copy = remote(weight_cols(to), wcol.at[me], w_send.at[d], w_recv.at[d], {"head": to})
            copy.start()
            sent.append(copy)

    own_w = pltpu.make_async_copy(weight_cols(me), wcol.at[me], own_sem.at[3])
    pairs_out()
    weights_out()
    forward_both(2, 1)
    forward_both(3, 1)

    m_ref[...] = jnp.full_like(m_ref, NEG)
    l_ref[...] = jnp.zeros_like(l_ref)
    acc_ref[...] = jnp.zeros_like(acc_ref)
    own_q.wait()
    for d in range(4):
        for dx in range(2):
            if d or dx:
                block = qg.at[(y + d) % NY, q_rows(x + dx)]
                remote(block, block, q_send.at[d, dx], q_recv.at[d, dx], at(y + d, z, x + dx)).wait_recv()

    def attend_later(yk, k, v):
        for case in range(NY - 1):

            @pl.when(yk == case)
            def _():
                attend(range(case + 1, NY), k(), v(), qg, m_ref, l_ref, acc_ref)

    def attend_single(yk, zk):
        attend_later(yk, lambda: kv[yk, zk, 0], lambda: kv[yk, zk, 1])

    def attend_same(yk, zk):
        @pl.when(zk < z)
        def _():
            attend([yk], kv[yk, zk, 0], kv[yk, zk, 1], qg, m_ref, l_ref, acc_ref)

    @pl.loop(0, NY)
    def _(j):
        pl.when(j == 2)(level_one)
        yk = y_of(j)
        attend_single(yk, z)
        key_at = lax.broadcasted_iota(jnp.int32, (tokens, wide), 0) + x * tokens
        seen = key_at <= lax.broadcasted_iota(jnp.int32, (tokens, wide), 1)
        attend([yk], kv[yk, z, 0], kv[yk, z, 1], qg, m_ref, l_ref, acc_ref, seen)

    stages = {2: level_two, 6: level_three}

    @pl.loop(0, 12)
    def _(n):
        j, hop = n % NY, n // NY + 1
        for when, stage in stages.items():
            pl.when(n == when)(stage)
        yk = y_of(j)
        before, after = (z - hop + NZ) % NZ, (z + hop) % NZ

        @pl.when(hop == 3)
        def _():
            arrive_up(j, 3)
            pl.when(j < 2)(lambda: upward(j, 3).start())
            arrive_down(j, 3)
            pl.when(j >= 2)(lambda: downward(j, 3).start())

        attend_later(
            yk,
            lambda: jnp.concatenate([kv[yk, before, 0], kv[yk, after, 0]], axis=0),
            lambda: jnp.concatenate([kv[yk, before, 1], kv[yk, after, 1]], axis=0),
        )
        attend_same(yk, before)
        attend_same(yk, after)

        @pl.when(hop == 1)
        def _():
            forward_both(j, 2)

    states_in()
    for h in range(HEADS):
        col = slice(h * HD, (h + 1) * HD)
        raw = mm_nt(qeff[:, col], sin[h]) + oloc[:, col]
        scaled = raw * lax.rsqrt(jnp.mean(raw * raw, axis=-1, keepdims=True) + EPSILON)
        normed[h] = scaled * dgain[...]

    @pl.loop(0, NY)
    def _(j):
        pl.when(j < 2)(lambda: arrive_up(j, 4))
        pl.when(j >= 2)(lambda: arrive_down(j, 4))
        yk = y_of(j)
        attend_single(yk, (z + 4) % NZ)
        attend_same(yk, (z + 4) % NZ)

    for d in (2, 1, 3, 0):
        t = (y + d) % NY
        total = l_ref[t]
        some = total > 0.0
        safe = jnp.where(some, total, 1.0)
        o[t] = (acc_ref[t] / safe).T.astype(BF16)
        level = jnp.where(some, m_ref[t] * (SCALE * LOG2E) + jnp.log2(safe), NEG)
        lse[t] = jnp.broadcast_to(level, (8, wide))
        for dx in range(2):
            if d or dx:
                to, back = at(t, z, x + dx), (NY - d) % NY
                copy = remote(
                    o.at[t, q_rows(x + dx)], o_recv.at[y, x], o_send_sem.at[d, dx], o_recv_sem.at[back, dx], to
                )
                copy.start()
                sent.append(copy)
                copy = remote(lse.at[t], lse_recv.at[y, x], l_send_sem.at[d, dx], l_recv_sem.at[back, dx], to)
                copy.start()
                sent.append(copy)
    o_recv[y, x] = o[y, q_rows(x), :]
    lse_recv[y, x] = lse[y]

    pick = (
        lax.broadcasted_iota(jnp.int32, (tokens, wide), 1)
        == lax.broadcasted_iota(jnp.int32, (tokens, wide), 0) + x * tokens
    ).astype(F32)
    first_half = lax.broadcasted_iota(jnp.int32, (8, wide), 0) < 4

    def piece_of(device, j):
        return comb.at[device, :, head_cols(y_of(j))]

    for j in range(NY):
        d = Y_ORDER[j]
        h = (y + d) % NY
        for dx in range(2):
            if d or dx:
                there = (x + dx) % NX
                block = o_recv.at[h, there]
                remote(block, block, o_send_sem.at[d, dx], o_recv_sem.at[d, dx], at(h, z, there)).wait_recv()
                block = lse_recv.at[h, there]
                remote(block, block, l_send_sem.at[d, dx], l_recv_sem.at[d, dx], at(h, z, there)).wait_recv()
        a, b = lse_recv[h, 0], lse_recv[h, 1]
        top = jnp.maximum(a, b)
        a, b = jnp.exp2(a - top), jnp.exp2(b - top)
        shares = mm_nt(pick, jnp.where(first_half, a, b) / (a + b), HIGHEST)
        raw = o_recv[h, 0].astype(F32) * shares[:, :1] + o_recv[h, 1].astype(F32) * shares[:, 4:5]
        scaled = raw * lax.rsqrt(jnp.mean(raw * raw, axis=-1, keepdims=True) + EPSILON)
        comb[me, :, head_cols(h)] = (0.5 * (normed[h] + scaled * again[...])).astype(BF16)
        for way, to in enumerate((facing, sibling)):
            copy = remote(piece_of(me, j), piece_of(me, j), ag_send.at[way, j], ag_recv.at[way, j], {"head": to})
            copy.start()
            sent.append(copy)

    def share(device):
        return jnp.dot(comb[device], wcol[device], preferred_element_type=F32)

    for j in range(NY):
        block = piece_of(facing, j)
        remote(block, block, ag_send.at[0, j], ag_recv.at[0, j], {"head": facing}).wait_recv()
        copy = remote(block, block, relay_send.at[j], relay_recv.at[j], {"head": sibling})
        copy.start()
        sent.append(copy)
    own_w.wait()
    for d in (1, 2, 3):
        block = wcol.at[(me - d + 4) % 4]
        remote(block, block, w_send.at[d], w_recv.at[d], {"head": (me + d) % 4}).wait_recv()
    total = share(me) + share(facing)
    for j in range(NY):
        block = piece_of(sibling, j)
        remote(block, block, ag_send.at[1, j], ag_recv.at[1, j], {"head": sibling}).wait_recv()
    total = total + share(sibling)
    for j in range(NY):
        block = piece_of(diagonal, j)
        remote(block, block, relay_send.at[j], relay_recv.at[j], {"head": sibling}).wait_recv()
    out[...] = total + share(diagonal)
    for copy in sent + exchange(1, t_buf, g, in_chain) + exchange(2, u_buf, y, in_column) + states_out():
        copy.wait_send()
    for j in range(NY):
        for hop in range(4):
            if hop < UP_HOPS[j]:
                upward(j, hop).wait_send()
            if hop < DOWN_HOPS[j]:
                downward(j, hop).wait_send()


VMEM = pl.BlockSpec(memory_space=pltpu.VMEM)
ANY = pl.BlockSpec(memory_space=pl.ANY)
DMA = pltpu.SemaphoreType.DMA
LIMIT = 60 * 1024 * 1024


def local(
    hidden_in, delta_q, delta_k, delta_v, beta, log_decay, resets,
    attn_q, attn_k, attn_v, delta_gain, attn_gain, out_weight,
):
    tokens, cols = delta_q.shape
    struct = jax.ShapeDtypeStruct
    wide = NX * tokens
    vmem = pltpu.VMEM
    shared = pl.pallas_call(
        main_kernel,
        out_shape=struct((tokens, cols), F32),
        in_specs=[ANY] * 12,
        out_specs=VMEM,
        scratch_shapes=[
            vmem((NY, wide, HD), BF16),
            vmem((NY, 8, wide), F32),
            vmem((HEADS, HD, HD), BF16),
            vmem((tokens, cols), F32),
            vmem((tokens, cols), BF16),
            vmem((1, HD), F32),
            vmem((1, HD), F32),
            vmem((HEADS, tokens, HD), F32),
            vmem((NY, NX, tokens, HD), BF16),
            vmem((NY, NX, 8, wide), F32),
            vmem((4, tokens, cols), BF16),
            vmem((4, cols, cols), BF16),
            vmem((tokens, cols), BF16), vmem((tokens, cols), BF16), vmem((tokens, cols), BF16),
            vmem((HEADS, tokens), F32), vmem((HEADS, tokens), F32), vmem((1, tokens), jnp.int32),
            vmem((16, tokens), F32),
            vmem((NY, NZ, 2, tokens, HD), BF16),
            vmem((NY, wide, HD), BF16),
            vmem((NY, 1, wide), F32),
            vmem((NY, 1, wide), F32),
            vmem((NY, HD, wide), F32),
            vmem((HEADS, 2, HD, HD), BF16),
            vmem((GROUP, 2, HD, HD), BF16),
            vmem((GROUP, 2, HD, HD), BF16),
            vmem((NY, 2, HD, HD), BF16),
            vmem((4, 2, HD, HD), F32),
            vmem((GROUP, HD, HD), BF16),
            DMA((8,)),
            DMA((4,)),
            DMA((4, 2)), DMA((4, 2)),
            DMA((4, 2)), DMA((4, 2)),
            DMA((4, 4)), DMA((4, 4)),
            DMA((4, 4)), DMA((4, 4)),
            DMA((4, 4)), DMA((4, 4)),
            DMA((4, 2)), DMA((4, 2)),
            DMA((4, 2)), DMA((4, 2)),
            DMA((4,)), DMA((4,)),
            DMA((2, 4)), DMA((2, 4)),
            DMA((4,)), DMA((4,)),
        ],
        compiler_params=pltpu.CompilerParams(
            collective_id=0, has_side_effects=True, vmem_limit_bytes=LIMIT
        ),
    )(
        delta_q, delta_k, delta_v, beta.T, log_decay.T, resets.reshape(1, tokens),
        attn_q, attn_k, attn_v, out_weight,
        delta_gain.reshape(1, HD), attn_gain.reshape(1, HD),
    )
    return (hidden_in.astype(F32) + shared).astype(BF16)


def solution(mesh):
    by_head = P("seq", "head")
    placed = (by_head,) * 6 + (P("seq"),) + (by_head,) * 3 + (P(), P(), P("head", None))
    return jax.shard_map(local, mesh=mesh, in_specs=placed, out_specs=by_head, check_vma=False)
```

```python
import jax
import jax.numpy as jnp
from jax import lax
from jax.experimental import pallas as pl
from jax.experimental.pallas import tpu as pltpu
from jax.sharding import PartitionSpec as P

HD = 128
EPSILON = 1e-06
NY, NZ, NX = 4, 8, 2
HEADS = 4
GROUP = 4
SUB = 64
MESH = pl.DeviceIdType.MESH
HIGHEST = lax.Precision.HIGHEST
F32 = jnp.float32
BF16 = jnp.bfloat16
NEG = -1e30
SCALE = HD**-0.5
LOG2E = 1.4426950408889634
Y_ORDER = (0, 1, 3, 2)
UP_HOPS = (4, 4, 3, 3)
DOWN_HOPS = (3, 3, 4, 4)


def mm(a, b):
    return jnp.dot(a.astype(BF16), b.astype(BF16), preferred_element_type=F32)


def mm_nt(a, b, precision=None):
    return lax.dot_general(
        a, b, (((1,), (1,)), ((), ())), precision=precision, preferred_element_type=F32
    )


def mm_tn(a, b):
    return lax.dot_general(
        a.astype(BF16), b.astype(BF16), (((0,), (0,)), ((), ())), preferred_element_type=F32
    )


def place():
    s = lax.axis_index("seq")
    return s // (NZ * NX), (s // NX) % NZ, s % NX


def at(y, z, x):
    return {"seq": ((y % NY) * NZ + z % NZ) * NX + x % NX}


def remote(src, dst, send, recv, device):
    return pltpu.make_async_remote_copy(
        src_ref=src,
        dst_ref=dst,
        send_sem=send,
        recv_sem=recv,
        device_id=device,
        device_id_type=MESH,
    )


def delta_head(h, dq, dk, dv, betas, cum_col, cum_row, oloc, qeff, ab_send):
    tokens = dq.shape[0]
    col = slice(h * HD, (h + 1) * HD)
    q = dq[:, col].astype(F32)
    k = dk[:, col].astype(F32)
    v = dv[:, col].astype(F32)
    q = q * (lax.rsqrt(jnp.sum(q * q, axis=-1, keepdims=True) + EPSILON) * SCALE)
    k = k * lax.rsqrt(jnp.sum(k * k, axis=-1, keepdims=True) + EPSILON)
    strength = betas[:, h + 8 : h + 9]
    row_id = lax.broadcasted_iota(jnp.int32, (tokens, tokens), 0)
    col_id = lax.broadcasted_iota(jnp.int32, (tokens, tokens), 1)
    c_col, n_col = cum_col[:, h : h + 1], cum_col[:, HEADS : HEADS + 1]
    c_row, n_row = cum_row[h : h + 1, :], cum_row[HEADS : HEADS + 1, :]
    reach = jnp.where(n_col < 0.5, jnp.exp(c_col), 0.0)
    same = (jnp.abs(n_col - n_row) < 0.5) & (row_id >= col_id)
    ratios = jnp.where(same, jnp.exp(jnp.minimum(c_col - c_row, 0.0)), 0.0)
    kb = k.astype(BF16)
    inner = mm_nt(kb, kb)
    system = jnp.where(row_id > col_id, strength * ratios * inner, 0.0)
    near = (row_id // SUB) == (col_id // SUB)
    power = jnp.where(near, -system, 0.0)
    far = jnp.where(near, 0.0, system)
    inverse = jnp.where(row_id == col_id, 1.0, power)
    reached = 2
    while reached < SUB:
        power = mm(power, power)
        inverse = inverse + mm(inverse, power)
        reached *= 2
    right = jnp.concatenate([strength * v, (strength * reach) * k], axis=1)
    solved = mm(inverse, right)
    spread = mm(inverse, far)
    total = solved
    for _ in range((tokens + SUB - 1) // SUB - 1):
        total = solved - mm(spread, total)
    n_last, c_last = n_col[tokens - 1 :, :], c_col[tokens - 1 :, :]
    tail = jnp.where(jnp.abs(n_col - n_last) < 0.5, jnp.exp(jnp.minimum(c_last - c_col, 0.0)), 0.0) * k
    moved = mm_tn(total, tail)
    eye = (row_id == col_id)[:HD, :HD]
    ab_send[h, 0] = (jnp.where(eye, reach[tokens - 1 :, :], 0.0) - moved[HD:]).astype(BF16)
    ab_send[h, 1] = moved[:HD].astype(BF16)
    seen = mm(mm_nt(q.astype(BF16), kb) * ratios, total)
    oloc[:, col] = seen[:, :HD]
    qeff[:, col] = (reach * q - seen[:, HD:]).astype(BF16)


def attend(first, tiles, k, v, q, m_ref, l_ref, acc_ref, seen=None):
    factor = SCALE * LOG2E
    wide = q.shape[1] // NY
    span = tiles * wide
    at_ = pl.ds(first * wide, span) if isinstance(first, int) else pl.ds(pl.multiple_of(first * wide, HD), span)
    s = jnp.dot(k, q[:, at_], preferred_element_type=F32)
    if seen is not None:
        s = jnp.where(seen, s, NEG)
    old = m_ref[:, at_]
    new = jnp.maximum(old, jnp.max(s, axis=0, keepdims=True))
    p = jnp.exp2((s - new) * factor)
    if seen is not None:
        p = jnp.where(seen, p, 0.0)
    shrink = jnp.exp2((old - new) * factor)
    l_ref[:, at_] = l_ref[:, at_] * shrink + jnp.sum(p, axis=0, keepdims=True)
    acc_ref[:, at_] = acc_ref[:, at_] * shrink + mm_tn(v, p)
    m_ref[:, at_] = new


def main_kernel(
    dq_in, dk_in, dv_in, beta_in, decay_in, resets_in, aq, ak, av, weight, dgain_in, again_in,
    out,
    o, lse, sin, oloc, qeff, dgain, again, normed, o_recv, lse_recv, comb, wcol,
    dq, dk, dv, beta, decay, resets, rows,
    kv, qg, qt, m_ref, l_ref, acc_ref,
    ab_send, ab_recv, t_buf, u_buf, e_buf, s_send,
    in_sem, own_sem, kv_send, kv_recv, q_send, q_recv, up_send, up_recv, down_send, down_recv,
    c_send, c_recv,
    o_send_sem, o_recv_sem, l_send_sem, l_recv_sem, w_send, w_recv, ag_send, ag_recv, relay_send, relay_recv,
):
    y, z, x = place()
    me = lax.axis_index("head")
    sibling, facing = me + 1 - 2 * (me % 2), (me + 2) % 4
    diagonal = (sibling + 2) % 4
    cols = dq.shape[1]
    r, g = (z % 2) * 2 + x, z // 2
    tokens = dq.shape[0]
    wide = NX * tokens
    loads = [
        pltpu.make_async_copy(a, b, in_sem.at[i])
        for i, (a, b) in enumerate(
            zip(
                (dq_in, dk_in, dv_in, beta_in, decay_in, resets_in, dgain_in, again_in),
                (dq, dk, dv, beta, decay, resets, dgain, again),
            )
        )
    ]
    for load in loads:
        load.start()
    across = z + 1 - 2 * (z % 2)
    beyond = z - 1 + 2 * (z % 2)
    peers = [at(y + d, z, x) for d in (1, 2, 3)]
    peers += [at(y + d, z, x + 1) for d in range(4)]
    peers += [at(y, across, x), at(y, across, x + 1), at(y, beyond, x)]
    peers += [at(y, z + d, x) for d in (2, 4, 6)]
    peers += [{"head": (me + d) % 4} for d in (1, 2, 3)]
    barrier = pltpu.get_barrier_semaphore()
    for peer in peers:
        pl.semaphore_signal(barrier, inc=1, device_id=peer, device_id_type=MESH)
    pl.semaphore_wait(barrier, len(peers))
    sent = []

    def head_cols(h):
        return pl.ds(pl.multiple_of((h % NY) * HD, HD), HD)

    def q_rows(xx):
        return pl.ds(pl.multiple_of((xx % NX) * tokens, 64), tokens)

    own_k = pltpu.make_async_copy(ak.at[:, head_cols(y)], kv.at[y, z, 0], own_sem.at[0])
    own_v = pltpu.make_async_copy(av.at[:, head_cols(y)], kv.at[y, z, 1], own_sem.at[1])
    own_q = pltpu.make_async_copy(aq.at[:, head_cols(y)], qg.at[y, q_rows(x)], own_sem.at[2])
    for send, recv, dz in ((up_send, up_recv, 1), (down_send, down_recv, NZ - 1)):
        for part, source in enumerate((ak, av)):
            remote(
                source.at[:, head_cols(y)], kv.at[y, z, part], send.at[0, 0], recv.at[0, 0], at(y, z + dz, x)
            ).start()
    own_k.start()
    own_v.start()
    for j in (1, 2, 3):
        to = y - Y_ORDER[j] + NY
        for part, source in enumerate((ak, av)):
            copy = remote(
                source.at[:, head_cols(to)], kv.at[y, z, part],
                kv_send.at[j, part], kv_recv.at[j, part], at(to, z, x),
            )
            copy.start()
            sent.append(copy)

    def y_of(j):
        step = Y_ORDER[j] if isinstance(j, int) else j + jnp.where(j == 2, 1, 0) - jnp.where(j == 3, 1, 0)
        return (y + step) % NY

    def upward(j, hop):
        block = kv.at[y_of(j), (z - hop + NZ) % NZ]
        return remote(block, block, up_send.at[j, hop], up_recv.at[j, hop], at(y, z + 1, x))

    def downward(j, hop):
        block = kv.at[y_of(j), (z + hop) % NZ]
        return remote(block, block, down_send.at[j, hop], down_recv.at[j, hop], at(y, z - 1 + NZ, x))

    def arrive_up(j, hop):
        block = kv.at[y_of(j), (z - hop + NZ) % NZ]
        remote(block, block, up_send.at[j, hop - 1], up_recv.at[j, hop - 1], at(y, z + 1, x)).wait_recv()

    def arrive_down(j, hop):
        block = kv.at[y_of(j), (z + hop) % NZ]
        remote(block, block, down_send.at[j, hop - 1], down_recv.at[j, hop - 1], at(y, z + 1, x)).wait_recv()

    own_q.start()
    for d in range(4):
        for dx in range(2):
            if d or dx:
                to = y + d
                copy = remote(
                    aq.at[:, head_cols(to)], qg.at[y, q_rows(x)],
                    q_send.at[d, dx], q_recv.at[(NY - d) % NY, dx], at(to, z, x + dx),
                )
                copy.start()
                sent.append(copy)

    for load in loads:
        load.wait()
    rows[...] = jnp.zeros_like(rows)
    rows[0:HEADS] = decay[...]
    rows[HEADS : HEADS + 1] = resets[...].astype(F32)
    rows[8 : 8 + HEADS] = beta[...]
    row_id = lax.broadcasted_iota(jnp.int32, (tokens, tokens), 0)
    col_id = lax.broadcasted_iota(jnp.int32, (tokens, tokens), 1)
    low = (row_id >= col_id).astype(F32)
    cum_col = mm_nt(low, rows[...], HIGHEST)
    cum_row = mm_nt(rows[...], low, HIGHEST)
    betas = mm_nt((row_id == col_id).astype(F32), rows[...], HIGHEST)

    def first_round(j):
        for part in range(2):
            block = kv.at[y_of(j), z, part]
            remote(block, block, kv_send.at[j, part], kv_recv.at[j, part], at(y + 1, z, x)).wait_recv()
        upward(j, 0).start()
        downward(j, 0).start()

    def forward_both(j, hop):
        arrive_up(j, hop)
        upward(j, hop).start()
        arrive_down(j, hop)
        downward(j, hop).start()

    def of_group(index):
        return at(y, g * 2 + (index % GROUP) // 2, (index % GROUP) % 2)

    def pair_copy(h):
        d = (h - r + GROUP) % GROUP
        return remote(ab_send.at[h], ab_recv.at[r], c_send.at[0, d], c_recv.at[0, d], of_group(h))

    for h in range(HEADS):
        delta_head(h, dq, dk, dv, betas, cum_col, cum_row, oloc, qeff, ab_send)
        pl.when(r != h)(lambda: pair_copy(h).start())
        if h:
            first_round(h)
        if h >= 2:
            forward_both(h - 2, 1)

    def pairs_in():
        for d in (1, 2, 3):
            block = ab_recv.at[(r - d + GROUP) % GROUP]
            remote(block, block, c_send.at[0, d], c_recv.at[0, d], of_group(r + 1)).wait_recv()

    def exchange(level, buf, mine, device):
        return [
            remote(buf.at[mine], buf.at[mine], c_send.at[level, d], c_recv.at[level, d], device(d))
            for d in (1, 2, 3)
        ]

    def exchange_in(level, buf, mine, device):
        for d in (1, 2, 3):
            block = buf.at[(mine - d + GROUP) % GROUP]
            remote(block, block, c_send.at[level, d], c_recv.at[level, d], device(d)).wait_recv()

    def fold(buf):
        a, b = [buf[i, 0] for i in range(GROUP)], [buf[i, 1].astype(F32) for i in range(GROUP)]

        def join(one, two):
            both = mm(jnp.concatenate([one[0].astype(BF16), one[1].astype(BF16)], axis=0), two[0])
            return both[:HD], both[HD:] + two[1]

        pairs = list(zip(a, b))
        early, late = join(pairs[0], pairs[1]), join(pairs[2], pairs[3])
        first = (a[0].astype(F32), b[0])
        return [first, early, join(early, pairs[2])], join(early, late)

    in_chain = lambda d: at(y, z + 2 * d, x)
    in_column = lambda d: at(y + d, z, x)

    def level_one():
        pairs_in()
        before, (a, b) = fold(ab_recv)
        for i, (ea, eb) in enumerate(before):
            e_buf[i, 0] = ea
            e_buf[i, 1] = eb
        t_buf[g, 0] = a.astype(BF16)
        t_buf[g, 1] = b.astype(BF16)
        for copy in exchange(1, t_buf, g, in_chain):
            copy.start()

    def level_two():
        exchange_in(1, t_buf, g, in_chain)
        before, (a, b) = fold(t_buf)
        eye = (row_id == col_id)[:HD, :HD].astype(F32)
        fa, fb = eye, jnp.zeros((HD, HD), F32)
        for i, (ea, eb) in enumerate(before):
            fa = jnp.where(g == i + 1, ea, fa)
            fb = jnp.where(g == i + 1, eb, fb)
        e_buf[3, 0] = fa
        e_buf[3, 1] = fb
        u_buf[y, 0] = a.astype(BF16)
        u_buf[y, 1] = b.astype(BF16)
        for copy in exchange(2, u_buf, y, in_column):
            copy.start()

    def states_out():
        copies = []
        for d in (1, 2, 3):
            to = (r + d) % GROUP
            copies.append(remote(s_send.at[to], sin.at[r], c_send.at[3, d], c_recv.at[3, d], of_group(to)))
        return copies

    def level_three():
        exchange_in(2, u_buf, y, in_column)
        state = jnp.zeros((HD, HD), F32)
        b = u_buf[0, 1].astype(F32)
        for i in range(1, NY):
            state = jnp.where(y == i, b, state)
            if i < NY - 1:
                b = mm(b, u_buf[i, 0]) + u_buf[i, 1].astype(F32)
        state = mm(state, e_buf[3, 0]) + e_buf[3, 1]
        s_send[0] = state.astype(BF16)
        for i in range(3):
            s_send[i + 1] = (mm(state, e_buf[i, 0]) + e_buf[i, 1]).astype(BF16)
        for copy in states_out():
            copy.start()
        sin[r] = s_send[r]

    def states_in():
        for d in (1, 2, 3):
            block = sin.at[(r - d + GROUP) % GROUP]
            remote(block, block, c_send.at[3, d], c_recv.at[3, d], of_group(r + 1)).wait_recv()

    def weight_cols(device):
        return weight.at[:, pl.ds(pl.multiple_of(device * cols, HD), cols)]

    def weights_out():
        own_w.start()
        for d in (1, 2, 3):
            to = (me + d) % 4
            copy = remote(weight_cols(to), wcol.at[me], w_send.at[d], w_recv.at[d], {"head": to})
            copy.start()
            sent.append(copy)

    own_w = pltpu.make_async_copy(weight_cols(me), wcol.at[me], own_sem.at[3])
    ab_recv[r] = ab_send[r]
    weights_out()
    forward_both(2, 1)
    forward_both(3, 1)

    m_ref[...] = jnp.full_like(m_ref, NEG)
    l_ref[...] = jnp.zeros_like(l_ref)
    acc_ref[...] = jnp.zeros_like(acc_ref)
    own_k.wait()
    own_v.wait()
    own_q.wait()
    for d in range(4):
        for dx in range(2):
            if d or dx:
                block = qg.at[(y + d) % NY, q_rows(x + dx)]
                remote(block, block, q_send.at[d, dx], q_recv.at[d, dx], at(y + d, z, x + dx)).wait_recv()

    for t in range(NY):
        qt[:, t * wide : (t + 1) * wide] = qg[t].T

    def attend_later(yk, k, v):
        for case in range(NY - 1):

            @pl.when(yk == case)
            def _():
                attend(case + 1, NY - 1 - case, k(), v(), qt, m_ref, l_ref, acc_ref)

    def attend_single(yk, zk):
        attend_later(yk, lambda: kv[yk, zk, 0], lambda: kv[yk, zk, 1])

    def attend_same(yk, zk):
        @pl.when(zk < z)
        def _():
            attend(yk, 1, kv[yk, zk, 0], kv[yk, zk, 1], qt, m_ref, l_ref, acc_ref)

    @pl.loop(0, NY)
    def _(j):
        yk = y_of(j)
        attend_single(yk, z)
        key_at = lax.broadcasted_iota(jnp.int32, (tokens, wide), 0) + x * tokens
        seen = key_at <= lax.broadcasted_iota(jnp.int32, (tokens, wide), 1)
        attend(yk, 1, kv[yk, z, 0], kv[yk, z, 1], qt, m_ref, l_ref, acc_ref, seen)

    stages = {0: level_one, 6: level_two, 9: level_three}

    @pl.loop(0, 12)
    def _(n):
        j, hop = n % NY, n // NY + 1
        for when, stage in stages.items():
            pl.when(n == when)(stage)
        yk = y_of(j)
        before, after = (z - hop + NZ) % NZ, (z + hop) % NZ

        @pl.when(hop == 3)
        def _():
            arrive_up(j, 3)
            pl.when(j < 2)(lambda: upward(j, 3).start())
            arrive_down(j, 3)
            pl.when(j >= 2)(lambda: downward(j, 3).start())

        attend_later(
            yk,
            lambda: jnp.concatenate([kv[yk, before, 0], kv[yk, after, 0]], axis=0),
            lambda: jnp.concatenate([kv[yk, before, 1], kv[yk, after, 1]], axis=0),
        )
        attend_same(yk, before)
        attend_same(yk, after)

        @pl.when(hop == 1)
        def _():
            forward_both(j, 2)

    @pl.loop(0, NY)
    def _(j):
        pl.when(j < 2)(lambda: arrive_up(j, 4))
        pl.when(j >= 2)(lambda: arrive_down(j, 4))
        yk = y_of(j)
        attend_single(yk, (z + 4) % NZ)
        attend_same(yk, (z + 4) % NZ)

    for d in (2, 1, 3, 0):
        t = (y + d) % NY
        tile = pl.ds(pl.multiple_of(t * wide, HD), wide)
        total = l_ref[:, tile]
        some = total > 0.0
        safe = jnp.where(some, total, 1.0)
        o[t] = (acc_ref[:, tile] * (1.0 / safe)).T.astype(BF16)
        level = jnp.where(some, m_ref[:, tile] * (SCALE * LOG2E) + jnp.log2(safe), NEG)
        lse[t] = jnp.broadcast_to(level, (8, wide))
        for dx in range(2):
            if d or dx:
                to, back = at(t, z, x + dx), (NY - d) % NY
                copy = remote(
                    o.at[t, q_rows(x + dx)], o_recv.at[y, x], o_send_sem.at[d, dx], o_recv_sem.at[back, dx], to
                )
                copy.start()
                sent.append(copy)
                copy = remote(lse.at[t], lse_recv.at[y, x], l_send_sem.at[d, dx], l_recv_sem.at[back, dx], to)
                copy.start()
                sent.append(copy)
    o_recv[y, x] = o[y, q_rows(x), :]
    lse_recv[y, x] = lse[y]

    states_in()
    for h in range(HEADS):
        col = slice(h * HD, (h + 1) * HD)
        raw = mm_nt(qeff[:, col], sin[h]) + oloc[:, col]
        scaled = raw * lax.rsqrt(jnp.mean(raw * raw, axis=-1, keepdims=True) + EPSILON)
        normed[h] = scaled * dgain[...]

    first_half = lax.broadcasted_iota(jnp.int32, (8, wide), 0) < 4

    def piece_of(device, j):
        return comb.at[device, :, head_cols(y_of(j))]

    for j in range(NY):
        d = Y_ORDER[j]
        h = (y + d) % NY
        for dx in range(2):
            if d or dx:
                there = (x + dx) % NX
                block = o_recv.at[h, there]
                remote(block, block, o_send_sem.at[d, dx], o_recv_sem.at[d, dx], at(h, z, there)).wait_recv()
                block = lse_recv.at[h, there]
                remote(block, block, l_send_sem.at[d, dx], l_recv_sem.at[d, dx], at(h, z, there)).wait_recv()
        a, b = lse_recv[h, 0], lse_recv[h, 1]
        top = jnp.maximum(a, b)
        a, b = jnp.exp2(a - top), jnp.exp2(b - top)
        shares = (jnp.where(first_half, a, b) / (a + b)).T
        shares = jnp.where(x == 0, shares[:tokens], shares[tokens:])
        raw = o_recv[h, 0].astype(F32) * shares[:, :1] + o_recv[h, 1].astype(F32) * shares[:, 4:5]
        scaled = raw * lax.rsqrt(jnp.mean(raw * raw, axis=-1, keepdims=True) + EPSILON)
        comb[me, :, head_cols(h)] = (0.5 * (normed[h] + scaled * again[...])).astype(BF16)
        for way, to in enumerate((facing, sibling)):
            copy = remote(piece_of(me, j), piece_of(me, j), ag_send.at[way, j], ag_recv.at[way, j], {"head": to})
            copy.start()
            sent.append(copy)

    def share(device):
        return jnp.dot(comb[device], wcol[device], preferred_element_type=F32)

    for j in range(NY):
        block = piece_of(facing, j)
        remote(block, block, ag_send.at[0, j], ag_recv.at[0, j], {"head": facing}).wait_recv()
        copy = remote(block, block, relay_send.at[j], relay_recv.at[j], {"head": sibling})
        copy.start()
        sent.append(copy)
    own_w.wait()
    for d in (1, 2, 3):
        block = wcol.at[(me - d + 4) % 4]
        remote(block, block, w_send.at[d], w_recv.at[d], {"head": (me + d) % 4}).wait_recv()
    total = share(me) + share(facing)
    for j in range(NY):
        block = piece_of(sibling, j)
        remote(block, block, ag_send.at[1, j], ag_recv.at[1, j], {"head": sibling}).wait_recv()
    total = total + share(sibling)
    for j in range(NY):
        block = piece_of(diagonal, j)
        remote(block, block, relay_send.at[j], relay_recv.at[j], {"head": sibling}).wait_recv()
    out[...] = total + share(diagonal)
    for d in (1, 2, 3):
        pair_copy((r + d) % GROUP).wait_send()
    for copy in sent + exchange(1, t_buf, g, in_chain) + exchange(2, u_buf, y, in_column) + states_out():
        copy.wait_send()
    for j in range(NY):
        for hop in range(4):
            if hop < UP_HOPS[j]:
                upward(j, hop).wait_send()
            if hop < DOWN_HOPS[j]:
                downward(j, hop).wait_send()


VMEM = pl.BlockSpec(memory_space=pltpu.VMEM)
ANY = pl.BlockSpec(memory_space=pl.ANY)
DMA = pltpu.SemaphoreType.DMA
LIMIT = 60 * 1024 * 1024


def local(
    hidden_in, delta_q, delta_k, delta_v, beta, log_decay, resets,
    attn_q, attn_k, attn_v, delta_gain, attn_gain, out_weight,
):
    tokens, cols = delta_q.shape
    struct = jax.ShapeDtypeStruct
    wide = NX * tokens
    vmem = pltpu.VMEM
    shared = pl.pallas_call(
        main_kernel,
        out_shape=struct((tokens, cols), F32),
        in_specs=[ANY] * 12,
        out_specs=VMEM,
        scratch_shapes=[
            vmem((NY, wide, HD), BF16),
            vmem((NY, 8, wide), F32),
            vmem((HEADS, HD, HD), BF16),
            vmem((tokens, cols), F32),
            vmem((tokens, cols), BF16),
            vmem((1, HD), F32),
            vmem((1, HD), F32),
            vmem((HEADS, tokens, HD), F32),
            vmem((NY, NX, tokens, HD), BF16),
            vmem((NY, NX, 8, wide), F32),
            vmem((4, tokens, cols), BF16),
            vmem((4, cols, cols), BF16),
            vmem((tokens, cols), BF16), vmem((tokens, cols), BF16), vmem((tokens, cols), BF16),
            vmem((HEADS, tokens), F32), vmem((HEADS, tokens), F32), vmem((1, tokens), jnp.int32),
            vmem((16, tokens), F32),
            vmem((NY, NZ, 2, tokens, HD), BF16),
            vmem((NY, wide, HD), BF16),
            vmem((HD, NY * wide), BF16),
            vmem((1, NY * wide), F32),
            vmem((1, NY * wide), F32),
            vmem((HD, NY * wide), F32),
            vmem((HEADS, 2, HD, HD), BF16),
            vmem((GROUP, 2, HD, HD), BF16),
            vmem((GROUP, 2, HD, HD), BF16),
            vmem((NY, 2, HD, HD), BF16),
            vmem((4, 2, HD, HD), F32),
            vmem((GROUP, HD, HD), BF16),
            DMA((8,)),
            DMA((4,)),
            DMA((4, 2)), DMA((4, 2)),
            DMA((4, 2)), DMA((4, 2)),
            DMA((4, 4)), DMA((4, 4)),
            DMA((4, 4)), DMA((4, 4)),
            DMA((4, 4)), DMA((4, 4)),
            DMA((4, 2)), DMA((4, 2)),
            DMA((4, 2)), DMA((4, 2)),
            DMA((4,)), DMA((4,)),
            DMA((2, 4)), DMA((2, 4)),
            DMA((4,)), DMA((4,)),
        ],
        compiler_params=pltpu.CompilerParams(
            collective_id=0, has_side_effects=True, vmem_limit_bytes=LIMIT
        ),
    )(
        delta_q, delta_k, delta_v, beta.T, log_decay.T, resets.reshape(1, tokens),
        attn_q, attn_k, attn_v, out_weight,
        delta_gain.reshape(1, HD), attn_gain.reshape(1, HD),
    )
    return (hidden_in.astype(F32) + shared).astype(BF16)


def solution(mesh):
    by_head = P("seq", "head")
    placed = (by_head,) * 6 + (P("seq"),) + (by_head,) * 3 + (P(), P(), P("head", None))
    return jax.shard_map(local, mesh=mesh, in_specs=placed, out_specs=by_head, check_vma=False)
```

```python
import jax
import jax.numpy as jnp
from jax import lax
from jax.experimental import pallas as pl
from jax.experimental.pallas import tpu as pltpu
from jax.sharding import PartitionSpec as P

HD = 128
EPSILON = 1e-06
NY, NZ, NX = 4, 8, 2
HEADS = 4
GROUP = 4
SUB = 64
MESH = pl.DeviceIdType.MESH
HIGHEST = lax.Precision.HIGHEST
F32 = jnp.float32
BF16 = jnp.bfloat16
NEG = -1e30
SCALE = HD**-0.5
LOG2E = 1.4426950408889634
Y_ORDER = (0, 1, 3, 2)
UP_HOPS = (4, 3, 4, 3)
DOWN_HOPS = (3, 4, 3, 4)


def mm(a, b):
    return jnp.dot(a.astype(BF16), b.astype(BF16), preferred_element_type=F32)


def mm_nt(a, b, precision=None):
    return lax.dot_general(
        a, b, (((1,), (1,)), ((), ())), precision=precision, preferred_element_type=F32
    )


def mm_tn(a, b):
    return lax.dot_general(
        a.astype(BF16), b.astype(BF16), (((0,), (0,)), ((), ())), preferred_element_type=F32
    )


def place():
    s = lax.axis_index("seq")
    return s // (NZ * NX), (s // NX) % NZ, s % NX


def at(y, z, x):
    return {"seq": ((y % NY) * NZ + z % NZ) * NX + x % NX}


def remote(src, dst, send, recv, device):
    return pltpu.make_async_remote_copy(
        src_ref=src,
        dst_ref=dst,
        send_sem=send,
        recv_sem=recv,
        device_id=device,
        device_id_type=MESH,
    )


def delta_head(h, dq, dk, dv, betas, cum_col, cum_row, oloc, qeff, ab_send):
    tokens = dq.shape[0]
    col = slice(h * HD, (h + 1) * HD)
    q = dq[:, col].astype(F32)
    k = dk[:, col].astype(F32)
    v = dv[:, col].astype(F32)
    q = q * (lax.rsqrt(jnp.sum(q * q, axis=-1, keepdims=True) + EPSILON) * SCALE)
    k = k * lax.rsqrt(jnp.sum(k * k, axis=-1, keepdims=True) + EPSILON)
    strength = betas[:, h + 8 : h + 9]
    row_id = lax.broadcasted_iota(jnp.int32, (tokens, tokens), 0)
    col_id = lax.broadcasted_iota(jnp.int32, (tokens, tokens), 1)
    c_col, n_col = cum_col[:, h : h + 1], cum_col[:, HEADS : HEADS + 1]
    c_row, n_row = cum_row[h : h + 1, :], cum_row[HEADS : HEADS + 1, :]
    reach = jnp.where(n_col < 0.5, jnp.exp(c_col), 0.0)
    same = (jnp.abs(n_col - n_row) < 0.5) & (row_id >= col_id)
    ratios = jnp.where(same, jnp.exp(jnp.minimum(c_col - c_row, 0.0)), 0.0)
    kb = k.astype(BF16)
    inner = mm_nt(kb, kb)
    system = jnp.where(row_id > col_id, strength * ratios * inner, 0.0)
    near = (row_id // SUB) == (col_id // SUB)
    power = jnp.where(near, -system, 0.0)
    far = jnp.where(near, 0.0, system)
    inverse = jnp.where(row_id == col_id, 1.0, power)
    reached = 2
    while reached < SUB:
        power = mm(power, power)
        inverse = inverse + mm(inverse, power)
        reached *= 2
    right = jnp.concatenate([strength * v, (strength * reach) * k], axis=1)
    solved = mm(inverse, right)
    spread = mm(inverse, far)
    total = solved
    for _ in range((tokens + SUB - 1) // SUB - 1):
        total = solved - mm(spread, total)
    n_last, c_last = n_col[tokens - 1 :, :], c_col[tokens - 1 :, :]
    tail = jnp.where(jnp.abs(n_col - n_last) < 0.5, jnp.exp(jnp.minimum(c_last - c_col, 0.0)), 0.0) * k
    moved = mm_tn(total, tail)
    eye = (row_id == col_id)[:HD, :HD]
    ab_send[h, 0] = (jnp.where(eye, reach[tokens - 1 :, :], 0.0) - moved[HD:]).astype(BF16)
    ab_send[h, 1] = moved[:HD].astype(BF16)
    seen = mm(mm_nt(q.astype(BF16), kb) * ratios, total)
    oloc[:, col] = seen[:, :HD]
    qeff[:, col] = (reach * q - seen[:, HD:]).astype(BF16)


def attend(first, tiles, k, v, q, m_ref, l_ref, acc_ref, seen=None):
    factor = SCALE * LOG2E
    wide = q.shape[1] // NY
    span = tiles * wide
    at_ = pl.ds(first * wide, span) if isinstance(first, int) else pl.ds(pl.multiple_of(first * wide, HD), span)
    s = jnp.dot(k, q[:, at_], preferred_element_type=F32)
    if seen is not None:
        s = jnp.where(seen, s, NEG)
    old = m_ref[:, at_]
    new = jnp.maximum(old, jnp.max(s, axis=0, keepdims=True))
    p = jnp.exp2((s - new) * factor)
    if seen is not None:
        p = jnp.where(seen, p, 0.0)
    shrink = jnp.exp2((old - new) * factor)
    l_ref[:, at_] = l_ref[:, at_] * shrink + jnp.sum(p, axis=0, keepdims=True)
    acc_ref[:, at_] = acc_ref[:, at_] * shrink + mm_tn(v, p)
    m_ref[:, at_] = new


def main_kernel(
    dq_in, dk_in, dv_in, beta_in, decay_in, resets_in, aq, ak, av, weight, dgain_in, again_in,
    out,
    o, lse, sin, oloc, qeff, dgain, again, normed, o_recv, lse_recv, comb, wcol,
    dq, dk, dv, beta, decay, resets, rows,
    kv, qg, qt, m_ref, l_ref, acc_ref,
    ab_send, ab_recv, t_buf, u_buf, e_buf, s_send,
    in_sem, own_sem, kv_send, kv_recv, q_send, q_recv, up_send, up_recv, down_send, down_recv,
    c_send, c_recv,
    o_send_sem, o_recv_sem, l_send_sem, l_recv_sem, w_send, w_recv, ag_send, ag_recv, relay_send, relay_recv,
):
    y, z, x = place()
    me = lax.axis_index("head")
    sibling, facing = me + 1 - 2 * (me % 2), (me + 2) % 4
    diagonal = (sibling + 2) % 4
    cols = dq.shape[1]
    r, g = (z % 2) * 2 + x, z // 2
    tokens = dq.shape[0]
    wide = NX * tokens
    loads = [
        pltpu.make_async_copy(a, b, in_sem.at[i])
        for i, (a, b) in enumerate(
            zip(
                (dq_in, dk_in, dv_in, beta_in, decay_in, resets_in, dgain_in, again_in),
                (dq, dk, dv, beta, decay, resets, dgain, again),
            )
        )
    ]
    for load in loads:
        load.start()
    across = z + 1 - 2 * (z % 2)
    beyond = z - 1 + 2 * (z % 2)
    peers = [at(y + d, z, x) for d in (1, 2, 3)]
    peers += [at(y + d, z, x + 1) for d in range(4)]
    peers += [at(y, across, x), at(y, across, x + 1), at(y, beyond, x)]
    peers += [at(y, z + d, x) for d in (2, 4, 6)]
    peers += [{"head": (me + d) % 4} for d in (1, 2, 3)]
    barrier = pltpu.get_barrier_semaphore()
    for peer in peers:
        pl.semaphore_signal(barrier, inc=1, device_id=peer, device_id_type=MESH)
    pl.semaphore_wait(barrier, len(peers))
    sent = []

    def head_cols(h):
        return pl.ds(pl.multiple_of((h % NY) * HD, HD), HD)

    def q_rows(xx):
        return pl.ds(pl.multiple_of((xx % NX) * tokens, 64), tokens)

    own_k = pltpu.make_async_copy(ak.at[:, head_cols(y)], kv.at[y, z, 0], own_sem.at[0])
    own_v = pltpu.make_async_copy(av.at[:, head_cols(y)], kv.at[y, z, 1], own_sem.at[1])
    own_q = pltpu.make_async_copy(aq.at[:, head_cols(y)], qg.at[y, q_rows(x)], own_sem.at[2])
    for send, recv, dz in ((up_send, up_recv, 1), (down_send, down_recv, NZ - 1)):
        for part, source in enumerate((ak, av)):
            remote(
                source.at[:, head_cols(y)], kv.at[y, z, part], send.at[y, 0], recv.at[y, 0], at(y, z + dz, x)
            ).start()
    own_k.start()
    own_v.start()
    for j in (1, 2, 3):
        to = y - Y_ORDER[j] + NY
        for part, source in enumerate((ak, av)):
            copy = remote(
                source.at[:, head_cols(to)], kv.at[y, z, part],
                kv_send.at[j, part], kv_recv.at[j, part], at(to, z, x),
            )
            copy.start()
            sent.append(copy)

    def y_of(j):
        return (y + Y_ORDER[j]) % NY

    def upward(j, hop):
        block = kv.at[j, (z - hop + NZ) % NZ]
        return remote(block, block, up_send.at[j, hop], up_recv.at[j, hop], at(y, z + 1, x))

    def downward(j, hop):
        block = kv.at[j, (z + hop) % NZ]
        return remote(block, block, down_send.at[j, hop], down_recv.at[j, hop], at(y, z - 1 + NZ, x))

    def arrive_up(j, hop):
        block = kv.at[j, (z - hop + NZ) % NZ]
        remote(block, block, up_send.at[j, hop - 1], up_recv.at[j, hop - 1], at(y, z + 1, x)).wait_recv()

    def arrive_down(j, hop):
        block = kv.at[j, (z + hop) % NZ]
        remote(block, block, down_send.at[j, hop - 1], down_recv.at[j, hop - 1], at(y, z + 1, x)).wait_recv()

    own_q.start()
    for d in range(4):
        for dx in range(2):
            if d or dx:
                to = y + d
                copy = remote(
                    aq.at[:, head_cols(to)], qg.at[y, q_rows(x)],
                    q_send.at[d, dx], q_recv.at[(NY - d) % NY, dx], at(to, z, x + dx),
                )
                copy.start()
                sent.append(copy)

    for load in loads:
        load.wait()
    rows[...] = jnp.zeros_like(rows)
    rows[0:HEADS] = decay[...]
    rows[HEADS : HEADS + 1] = resets[...].astype(F32)
    rows[8 : 8 + HEADS] = beta[...]
    row_id = lax.broadcasted_iota(jnp.int32, (tokens, tokens), 0)
    col_id = lax.broadcasted_iota(jnp.int32, (tokens, tokens), 1)
    low = (row_id >= col_id).astype(F32)
    cum_col = mm_nt(low, rows[...], HIGHEST)
    cum_row = mm_nt(rows[...], low, HIGHEST)
    betas = mm_nt((row_id == col_id).astype(F32), rows[...], HIGHEST)

    def first_round(j):
        for part in range(2):
            block = kv.at[y_of(j), z, part]
            remote(block, block, kv_send.at[j, part], kv_recv.at[j, part], at(y + 1, z, x)).wait_recv()
        upward(y_of(j), 0).start()
        downward(y_of(j), 0).start()

    def forward_both(j, hop):
        arrive_up(j, hop)
        upward(j, hop).start()
        arrive_down(j, hop)
        downward(j, hop).start()

    def of_group(index):
        return at(y, g * 2 + (index % GROUP) // 2, (index % GROUP) % 2)

    def pair_copy(h):
        d = (h - r + GROUP) % GROUP
        return remote(ab_send.at[h], ab_recv.at[r], c_send.at[0, d], c_recv.at[0, d], of_group(h))

    for h in range(HEADS):
        delta_head(h, dq, dk, dv, betas, cum_col, cum_row, oloc, qeff, ab_send)
        pl.when(r != h)(lambda: pair_copy(h).start())
        if h:
            first_round(h)

    def pairs_in():
        for d in (1, 2, 3):
            block = ab_recv.at[(r - d + GROUP) % GROUP]
            remote(block, block, c_send.at[0, d], c_recv.at[0, d], of_group(r + 1)).wait_recv()

    def exchange(level, buf, mine, device):
        return [
            remote(buf.at[mine], buf.at[mine], c_send.at[level, d], c_recv.at[level, d], device(d))
            for d in (1, 2, 3)
        ]

    def exchange_in(level, buf, mine, device):
        for d in (1, 2, 3):
            block = buf.at[(mine - d + GROUP) % GROUP]
            remote(block, block, c_send.at[level, d], c_recv.at[level, d], device(d)).wait_recv()

    def fold(buf):
        a, b = [buf[i, 0] for i in range(GROUP)], [buf[i, 1].astype(F32) for i in range(GROUP)]

        def join(one, two):
            both = mm(jnp.concatenate([one[0].astype(BF16), one[1].astype(BF16)], axis=0), two[0])
            return both[:HD], both[HD:] + two[1]

        pairs = list(zip(a, b))
        early, late = join(pairs[0], pairs[1]), join(pairs[2], pairs[3])
        first = (a[0].astype(F32), b[0])
        return [first, early, join(early, pairs[2])], join(early, late)

    in_chain = lambda d: at(y, z + 2 * d, x)
    in_column = lambda d: at(y + d, z, x)

    def level_one():
        pairs_in()
        before, (a, b) = fold(ab_recv)
        for i, (ea, eb) in enumerate(before):
            e_buf[i, 0] = ea
            e_buf[i, 1] = eb
        t_buf[g, 0] = a.astype(BF16)
        t_buf[g, 1] = b.astype(BF16)
        for copy in exchange(1, t_buf, g, in_chain):
            copy.start()

    def level_two():
        exchange_in(1, t_buf, g, in_chain)
        before, (a, b) = fold(t_buf)
        eye = (row_id == col_id)[:HD, :HD].astype(F32)
        fa, fb = eye, jnp.zeros((HD, HD), F32)
        for i, (ea, eb) in enumerate(before):
            fa = jnp.where(g == i + 1, ea, fa)
            fb = jnp.where(g == i + 1, eb, fb)
        e_buf[3, 0] = fa
        e_buf[3, 1] = fb
        u_buf[y, 0] = a.astype(BF16)
        u_buf[y, 1] = b.astype(BF16)
        for copy in exchange(2, u_buf, y, in_column):
            copy.start()

    def states_out():
        copies = []
        for d in (1, 2, 3):
            to = (r + d) % GROUP
            copies.append(remote(s_send.at[to], sin.at[r], c_send.at[3, d], c_recv.at[3, d], of_group(to)))
        return copies

    def level_three():
        exchange_in(2, u_buf, y, in_column)
        state = jnp.zeros((HD, HD), F32)
        b = u_buf[0, 1].astype(F32)
        for i in range(1, NY):
            state = jnp.where(y == i, b, state)
            if i < NY - 1:
                b = mm(b, u_buf[i, 0]) + u_buf[i, 1].astype(F32)
        state = mm(state, e_buf[3, 0]) + e_buf[3, 1]
        s_send[0] = state.astype(BF16)
        for i in range(3):
            s_send[i + 1] = (mm(state, e_buf[i, 0]) + e_buf[i, 1]).astype(BF16)
        for copy in states_out():
            copy.start()
        sin[r] = s_send[r]

    def states_in():
        for d in (1, 2, 3):
            block = sin.at[(r - d + GROUP) % GROUP]
            remote(block, block, c_send.at[3, d], c_recv.at[3, d], of_group(r + 1)).wait_recv()

    def weight_cols(device):
        return weight.at[:, pl.ds(pl.multiple_of(device * cols, HD), cols)]

    def weights_out():
        own_w.start()
        for d in (1, 2, 3):
            to = (me + d) % 4
            copy = remote(weight_cols(to), wcol.at[me], w_send.at[d], w_recv.at[d], {"head": to})
            copy.start()
            sent.append(copy)

    own_w = pltpu.make_async_copy(weight_cols(me), wcol.at[me], own_sem.at[3])
    ab_recv[r] = ab_send[r]
    weights_out()
    for yk in range(NY):
        forward_both(yk, 1)

    m_ref[...] = jnp.full_like(m_ref, NEG)
    l_ref[...] = jnp.zeros_like(l_ref)
    acc_ref[...] = jnp.zeros_like(acc_ref)
    own_k.wait()
    own_v.wait()
    own_q.wait()
    for d in range(4):
        for dx in range(2):
            if d or dx:
                block = qg.at[(y + d) % NY, q_rows(x + dx)]
                remote(block, block, q_send.at[d, dx], q_recv.at[d, dx], at(y + d, z, x + dx)).wait_recv()

    for t in range(NY):
        qt[:, t * wide : (t + 1) * wide] = qg[t].T

    def attend_later(yk, k, v):
        for case in range(NY - 1):

            @pl.when(yk == case)
            def _():
                attend(case + 1, NY - 1 - case, k(), v(), qt, m_ref, l_ref, acc_ref)

    def attend_single(yk, zk):
        attend_later(yk, lambda: kv[yk, zk, 0], lambda: kv[yk, zk, 1])

    def attend_same(yk, zk):
        @pl.when(zk < z)
        def _():
            attend(yk, 1, kv[yk, zk, 0], kv[yk, zk, 1], qt, m_ref, l_ref, acc_ref)

    @pl.loop(0, NY)
    def _(yk):
        attend_single(yk, z)
        key_at = lax.broadcasted_iota(jnp.int32, (tokens, wide), 0) + x * tokens
        seen = key_at <= lax.broadcasted_iota(jnp.int32, (tokens, wide), 1)
        attend(yk, 1, kv[yk, z, 0], kv[yk, z, 1], qt, m_ref, l_ref, acc_ref, seen)

    stages = {0: level_one, 6: level_two, 9: level_three}

    @pl.loop(0, 12)
    def _(n):
        yk, hop = n % NY, n // NY + 1
        for when, stage in stages.items():
            pl.when(n == when)(stage)
        before, after = (z - hop + NZ) % NZ, (z + hop) % NZ

        @pl.when(hop == 3)
        def _():
            arrive_up(yk, 3)
            pl.when(yk % 2 == 0)(lambda: upward(yk, 3).start())
            arrive_down(yk, 3)
            pl.when(yk % 2 == 1)(lambda: downward(yk, 3).start())

        attend_later(
            yk,
            lambda: jnp.concatenate([kv[yk, before, 0], kv[yk, after, 0]], axis=0),
            lambda: jnp.concatenate([kv[yk, before, 1], kv[yk, after, 1]], axis=0),
        )
        attend_same(yk, before)
        attend_same(yk, after)

        @pl.when(hop == 1)
        def _():
            forward_both(yk, 2)

    def tile_copies(t):
        d = (t - y + NY) % NY
        for xx in range(NX):
            dx, to, back = (xx - x + NX) % NX, at(t, z, xx), (NY - d) % NY
            rows_of = slice(xx * tokens, (xx + 1) * tokens)
            elsewhere = (t != y) | (xx != x)
            yield elsewhere, (
                remote(o.at[t, rows_of], o_recv.at[y, x], o_send_sem.at[d, dx], o_recv_sem.at[back, dx], to),
                remote(lse.at[t], lse_recv.at[y, x], l_send_sem.at[d, dx], l_recv_sem.at[back, dx], to),
            )

    opposite = (z + 4) % NZ
    for t in range(NY):
        (arrive_up if t % 2 == 0 else arrive_down)(t, 4)
        if t < NY - 1:
            attend(t + 1, NY - 1 - t, kv[t, opposite, 0], kv[t, opposite, 1], qt, m_ref, l_ref, acc_ref)
        attend_same(t, opposite)
        tile = slice(t * wide, (t + 1) * wide)
        total = l_ref[:, tile]
        some = total > 0.0
        safe = jnp.where(some, total, 1.0)
        o[t] = (acc_ref[:, tile] * (1.0 / safe)).T.astype(BF16)
        level = jnp.where(some, m_ref[:, tile] * (SCALE * LOG2E) + jnp.log2(safe), NEG)
        lse[t] = jnp.broadcast_to(level, (8, wide))
        for elsewhere, copies in tile_copies(t):

            @pl.when(elsewhere)
            def _():
                for copy in copies:
                    copy.start()

    o_recv[y, x] = o[y, q_rows(x), :]
    lse_recv[y, x] = lse[y]

    states_in()
    for h in range(HEADS):
        col = slice(h * HD, (h + 1) * HD)
        raw = mm_nt(qeff[:, col], sin[h]) + oloc[:, col]
        scaled = raw * lax.rsqrt(jnp.mean(raw * raw, axis=-1, keepdims=True) + EPSILON)
        normed[h] = scaled * dgain[...]

    first_half = lax.broadcasted_iota(jnp.int32, (8, wide), 0) < 4

    def piece_of(device, j):
        return comb.at[device, :, head_cols(y_of(j))]

    for j in range(NY):
        d = Y_ORDER[j]
        h = (y + d) % NY
        for dx in range(2):
            if d or dx:
                there = (x + dx) % NX
                block = o_recv.at[h, there]
                remote(block, block, o_send_sem.at[d, dx], o_recv_sem.at[d, dx], at(h, z, there)).wait_recv()
                block = lse_recv.at[h, there]
                remote(block, block, l_send_sem.at[d, dx], l_recv_sem.at[d, dx], at(h, z, there)).wait_recv()
        a, b = lse_recv[h, 0], lse_recv[h, 1]
        top = jnp.maximum(a, b)
        a, b = jnp.exp2(a - top), jnp.exp2(b - top)
        shares = (jnp.where(first_half, a, b) / (a + b)).T
        shares = jnp.where(x == 0, shares[:tokens], shares[tokens:])
        raw = o_recv[h, 0].astype(F32) * shares[:, :1] + o_recv[h, 1].astype(F32) * shares[:, 4:5]
        scaled = raw * lax.rsqrt(jnp.mean(raw * raw, axis=-1, keepdims=True) + EPSILON)
        comb[me, :, head_cols(h)] = (0.5 * (normed[h] + scaled * again[...])).astype(BF16)
        for way, to in enumerate((facing, sibling)):
            copy = remote(piece_of(me, j), piece_of(me, j), ag_send.at[way, j], ag_recv.at[way, j], {"head": to})
            copy.start()
            sent.append(copy)

    def share(device):
        return jnp.dot(comb[device], wcol[device], preferred_element_type=F32)

    for j in range(NY):
        block = piece_of(facing, j)
        remote(block, block, ag_send.at[0, j], ag_recv.at[0, j], {"head": facing}).wait_recv()
        copy = remote(block, block, relay_send.at[j], relay_recv.at[j], {"head": sibling})
        copy.start()
        sent.append(copy)
    own_w.wait()
    for d in (1, 2, 3):
        block = wcol.at[(me - d + 4) % 4]
        remote(block, block, w_send.at[d], w_recv.at[d], {"head": (me + d) % 4}).wait_recv()
    total = share(me) + share(facing)
    for j in range(NY):
        block = piece_of(sibling, j)
        remote(block, block, ag_send.at[1, j], ag_recv.at[1, j], {"head": sibling}).wait_recv()
    total = total + share(sibling)
    for j in range(NY):
        block = piece_of(diagonal, j)
        remote(block, block, relay_send.at[j], relay_recv.at[j], {"head": sibling}).wait_recv()
    out[...] = total + share(diagonal)
    for d in (1, 2, 3):
        pair_copy((r + d) % GROUP).wait_send()
    for t in range(NY):
        for elsewhere, copies in tile_copies(t):

            @pl.when(elsewhere)
            def _():
                for copy in copies:
                    copy.wait_send()

    for copy in sent + exchange(1, t_buf, g, in_chain) + exchange(2, u_buf, y, in_column) + states_out():
        copy.wait_send()
    for j in range(NY):
        for hop in range(4):
            if hop < UP_HOPS[j]:
                upward(j, hop).wait_send()
            if hop < DOWN_HOPS[j]:
                downward(j, hop).wait_send()


VMEM = pl.BlockSpec(memory_space=pltpu.VMEM)
ANY = pl.BlockSpec(memory_space=pl.ANY)
DMA = pltpu.SemaphoreType.DMA
LIMIT = 60 * 1024 * 1024


def local(
    hidden_in, delta_q, delta_k, delta_v, beta, log_decay, resets,
    attn_q, attn_k, attn_v, delta_gain, attn_gain, out_weight,
):
    tokens, cols = delta_q.shape
    struct = jax.ShapeDtypeStruct
    wide = NX * tokens
    vmem = pltpu.VMEM
    shared = pl.pallas_call(
        main_kernel,
        out_shape=struct((tokens, cols), F32),
        in_specs=[ANY] * 12,
        out_specs=VMEM,
        scratch_shapes=[
            vmem((NY, wide, HD), BF16),
            vmem((NY, 8, wide), F32),
            vmem((HEADS, HD, HD), BF16),
            vmem((tokens, cols), F32),
            vmem((tokens, cols), BF16),
            vmem((1, HD), F32),
            vmem((1, HD), F32),
            vmem((HEADS, tokens, HD), F32),
            vmem((NY, NX, tokens, HD), BF16),
            vmem((NY, NX, 8, wide), F32),
            vmem((4, tokens, cols), BF16),
            vmem((4, cols, cols), BF16),
            vmem((tokens, cols), BF16), vmem((tokens, cols), BF16), vmem((tokens, cols), BF16),
            vmem((HEADS, tokens), F32), vmem((HEADS, tokens), F32), vmem((1, tokens), jnp.int32),
            vmem((16, tokens), F32),
            vmem((NY, NZ, 2, tokens, HD), BF16),
            vmem((NY, wide, HD), BF16),
            vmem((HD, NY * wide), BF16),
            vmem((1, NY * wide), F32),
            vmem((1, NY * wide), F32),
            vmem((HD, NY * wide), F32),
            vmem((HEADS, 2, HD, HD), BF16),
            vmem((GROUP, 2, HD, HD), BF16),
            vmem((GROUP, 2, HD, HD), BF16),
            vmem((NY, 2, HD, HD), BF16),
            vmem((4, 2, HD, HD), F32),
            vmem((GROUP, HD, HD), BF16),
            DMA((8,)),
            DMA((4,)),
            DMA((4, 2)), DMA((4, 2)),
            DMA((4, 2)), DMA((4, 2)),
            DMA((4, 4)), DMA((4, 4)),
            DMA((4, 4)), DMA((4, 4)),
            DMA((4, 4)), DMA((4, 4)),
            DMA((4, 2)), DMA((4, 2)),
            DMA((4, 2)), DMA((4, 2)),
            DMA((4,)), DMA((4,)),
            DMA((2, 4)), DMA((2, 4)),
            DMA((4,)), DMA((4,)),
        ],
        compiler_params=pltpu.CompilerParams(
            collective_id=0, has_side_effects=True, vmem_limit_bytes=LIMIT
        ),
    )(
        delta_q, delta_k, delta_v, beta.T, log_decay.T, resets.reshape(1, tokens),
        attn_q, attn_k, attn_v, out_weight,
        delta_gain.reshape(1, HD), attn_gain.reshape(1, HD),
    )
    return (hidden_in.astype(F32) + shared).astype(BF16)


def solution(mesh):
    by_head = P("seq", "head")
    placed = (by_head,) * 6 + (P("seq"),) + (by_head,) * 3 + (P(), P(), P("head", None))
    return jax.shard_map(local, mesh=mesh, in_specs=placed, out_specs=by_head, check_vma=False)
```

```python
import jax
import jax.numpy as jnp
from jax import lax
from jax.experimental import pallas as pl
from jax.experimental.pallas import tpu as pltpu
from jax.sharding import PartitionSpec as P

HD = 128
EPSILON = 1e-06
NY, NZ, NX = 4, 8, 2
HEADS = 4
GROUP = 4
SUB = 64
MESH = pl.DeviceIdType.MESH
HIGHEST = lax.Precision.HIGHEST
F32 = jnp.float32
BF16 = jnp.bfloat16
NEG = -1e30
SCALE = HD**-0.5
LOG2E = 1.4426950408889634
Y_ORDER = (0, 1, 3, 2)
UP_HOPS = (4, 3, 4, 3)
DOWN_HOPS = (3, 4, 3, 4)


def mm(a, b):
    return jnp.dot(a.astype(BF16), b.astype(BF16), preferred_element_type=F32)


def mm_nt(a, b, precision=None):
    return lax.dot_general(
        a, b, (((1,), (1,)), ((), ())), precision=precision, preferred_element_type=F32
    )


def mm_tn(a, b):
    return lax.dot_general(
        a.astype(BF16), b.astype(BF16), (((0,), (0,)), ((), ())), preferred_element_type=F32
    )


def place():
    s = lax.axis_index("seq")
    return s // (NZ * NX), (s // NX) % NZ, s % NX


def at(y, z, x):
    return {"seq": ((y % NY) * NZ + z % NZ) * NX + x % NX}


def remote(src, dst, send, recv, device):
    return pltpu.make_async_remote_copy(
        src_ref=src,
        dst_ref=dst,
        send_sem=send,
        recv_sem=recv,
        device_id=device,
        device_id_type=MESH,
    )


def delta_head(h, dq, dk, dv, betas, cum_col, cum_row, oloc, qeff, ab_send):
    tokens = dq.shape[0]
    col = slice(h * HD, (h + 1) * HD)
    q = dq[:, col].astype(F32)
    k = dk[:, col].astype(F32)
    v = dv[:, col].astype(F32)
    q = q * (lax.rsqrt(jnp.sum(q * q, axis=-1, keepdims=True) + EPSILON) * SCALE)
    k = k * lax.rsqrt(jnp.sum(k * k, axis=-1, keepdims=True) + EPSILON)
    strength = betas[:, h + 8 : h + 9]
    row_id = lax.broadcasted_iota(jnp.int32, (tokens, tokens), 0)
    col_id = lax.broadcasted_iota(jnp.int32, (tokens, tokens), 1)
    c_col, n_col = cum_col[:, h : h + 1], cum_col[:, HEADS : HEADS + 1]
    c_row, n_row = cum_row[h : h + 1, :], cum_row[HEADS : HEADS + 1, :]
    reach = jnp.where(n_col < 0.5, jnp.exp(c_col), 0.0)
    same = (jnp.abs(n_col - n_row) < 0.5) & (row_id >= col_id)
    ratios = jnp.where(same, jnp.exp(jnp.minimum(c_col - c_row, 0.0)), 0.0)
    kb = k.astype(BF16)
    inner = mm_nt(kb, kb)
    system = jnp.where(row_id > col_id, strength * ratios * inner, 0.0)
    near = (row_id // SUB) == (col_id // SUB)
    power = jnp.where(near, -system, 0.0)
    far = jnp.where(near, 0.0, system)
    inverse = jnp.where(row_id == col_id, 1.0, power)
    reached = 2
    while reached < SUB:
        power = mm(power, power)
        inverse = inverse + mm(inverse, power)
        reached *= 2
    right = jnp.concatenate([strength * v, (strength * reach) * k], axis=1)
    solved = mm(inverse, right)
    spread = mm(inverse, far)
    total = solved
    for _ in range((tokens + SUB - 1) // SUB - 1):
        total = solved - mm(spread, total)
    n_last, c_last = n_col[tokens - 1 :, :], c_col[tokens - 1 :, :]
    tail = jnp.where(jnp.abs(n_col - n_last) < 0.5, jnp.exp(jnp.minimum(c_last - c_col, 0.0)), 0.0) * k
    moved = mm_tn(total, tail)
    eye = (row_id == col_id)[:HD, :HD]
    ab_send[h, 0] = (jnp.where(eye, reach[tokens - 1 :, :], 0.0) - moved[HD:]).astype(BF16)
    ab_send[h, 1] = moved[:HD].astype(BF16)
    seen = mm(mm_nt(q.astype(BF16), kb) * ratios, total)
    oloc[:, col] = seen[:, :HD]
    qeff[:, col] = (reach * q - seen[:, HD:]).astype(BF16)


def attend(first, tiles, k, v, q, m_ref, l_ref, acc_ref, seen=None):
    factor = SCALE * LOG2E
    wide = q.shape[1] // NY
    span = tiles * wide
    at_ = pl.ds(first * wide, span) if isinstance(first, int) else pl.ds(pl.multiple_of(first * wide, HD), span)
    s = jnp.dot(k, q[:, at_], preferred_element_type=F32)
    if seen is not None:
        s = jnp.where(seen, s, NEG)
    old = m_ref[:, at_]
    new = jnp.maximum(old, jnp.max(s, axis=0, keepdims=True))
    p = jnp.exp2((s - new) * factor)
    if seen is not None:
        p = jnp.where(seen, p, 0.0)
    shrink = jnp.exp2((old - new) * factor)
    l_ref[:, at_] = l_ref[:, at_] * shrink + jnp.sum(p, axis=0, keepdims=True)
    acc_ref[:, at_] = acc_ref[:, at_] * shrink + mm_tn(v, p)
    m_ref[:, at_] = new


def main_kernel(
    dq_in, dk_in, dv_in, beta_in, decay_in, resets_in, aq, ak, av, weight, dgain_in, again_in,
    out,
    o, lse, sin, oloc, qeff, dgain, again, normed, o_recv, lse_recv, comb, wcol,
    dq, dk, dv, beta, decay, resets, rows,
    kv, qg, qt, m_ref, l_ref, acc_ref,
    ab_send, ab_recv, t_buf, u_buf, e_buf, s_send,
    in_sem, own_sem, kv_send, kv_recv, q_send, q_recv, up_send, up_recv, down_send, down_recv,
    c_send, c_recv,
    o_send_sem, o_recv_sem, l_send_sem, l_recv_sem, w_send, w_recv, ag_send, ag_recv, relay_send, relay_recv,
):
    y, z, x = place()
    me = lax.axis_index("head")
    sibling, facing = me + 1 - 2 * (me % 2), (me + 2) % 4
    diagonal = (sibling + 2) % 4
    cols = dq.shape[1]
    r, g = (z % 2) * 2 + x, z // 2
    tokens = dq.shape[0]
    wide = NX * tokens
    loads = [
        pltpu.make_async_copy(a, b, in_sem.at[i])
        for i, (a, b) in enumerate(
            zip(
                (dq_in, dk_in, dv_in, beta_in, decay_in, resets_in, dgain_in, again_in),
                (dq, dk, dv, beta, decay, resets, dgain, again),
            )
        )
    ]
    for load in loads:
        load.start()
    across = z + 1 - 2 * (z % 2)
    beyond = z - 1 + 2 * (z % 2)
    peers = [at(y + d, z, x) for d in (1, 2, 3)]
    peers += [at(y + d, z, x + 1) for d in range(4)]
    peers += [at(y, across, x), at(y, across, x + 1), at(y, beyond, x)]
    peers += [at(y, z + d, x) for d in (2, 4, 6)]
    peers += [{"head": (me + d) % 4} for d in (1, 2, 3)]
    barrier = pltpu.get_barrier_semaphore()
    for peer in peers:
        pl.semaphore_signal(barrier, inc=1, device_id=peer, device_id_type=MESH)
    pl.semaphore_wait(barrier, len(peers))
    sent = []

    def head_cols(h):
        return pl.ds(pl.multiple_of((h % NY) * HD, HD), HD)

    def q_rows(xx):
        return pl.ds(pl.multiple_of((xx % NX) * tokens, 64), tokens)

    own_k = pltpu.make_async_copy(ak.at[:, head_cols(y)], kv.at[y, z, 0], own_sem.at[0])
    own_v = pltpu.make_async_copy(av.at[:, head_cols(y)], kv.at[y, z, 1], own_sem.at[1])
    own_q = pltpu.make_async_copy(aq.at[:, head_cols(y)], qg.at[y, q_rows(x)], own_sem.at[2])
    for send, recv, dz in ((up_send, up_recv, 1), (down_send, down_recv, NZ - 1)):
        for part, source in enumerate((ak, av)):
            remote(
                source.at[:, head_cols(y)], kv.at[y, z, part], send.at[y, 0], recv.at[y, 0], at(y, z + dz, x)
            ).start()
    own_k.start()
    own_v.start()
    for j in (1, 2, 3):
        to = y - Y_ORDER[j] + NY
        for part, source in enumerate((ak, av)):
            copy = remote(
                source.at[:, head_cols(to)], kv.at[y, z, part],
                kv_send.at[j, part], kv_recv.at[j, part], at(to, z, x),
            )
            copy.start()
            sent.append(copy)

    def y_of(j):
        return (y + Y_ORDER[j]) % NY

    def upward(j, hop):
        block = kv.at[j, (z - hop + NZ) % NZ]
        return remote(block, block, up_send.at[j, hop], up_recv.at[j, hop], at(y, z + 1, x))

    def downward(j, hop):
        block = kv.at[j, (z + hop) % NZ]
        return remote(block, block, down_send.at[j, hop], down_recv.at[j, hop], at(y, z - 1 + NZ, x))

    def arrive_up(j, hop):
        block = kv.at[j, (z - hop + NZ) % NZ]
        remote(block, block, up_send.at[j, hop - 1], up_recv.at[j, hop - 1], at(y, z + 1, x)).wait_recv()

    def arrive_down(j, hop):
        block = kv.at[j, (z + hop) % NZ]
        remote(block, block, down_send.at[j, hop - 1], down_recv.at[j, hop - 1], at(y, z + 1, x)).wait_recv()

    own_q.start()
    for d in range(4):
        for dx in range(2):
            if d or dx:
                to = y + d
                copy = remote(
                    aq.at[:, head_cols(to)], qg.at[y, q_rows(x)],
                    q_send.at[d, dx], q_recv.at[(NY - d) % NY, dx], at(to, z, x + dx),
                )
                copy.start()
                sent.append(copy)

    for load in loads:
        load.wait()
    rows[...] = jnp.zeros_like(rows)
    rows[0:HEADS] = decay[...]
    rows[HEADS : HEADS + 1] = resets[...].astype(F32)
    rows[8 : 8 + HEADS] = beta[...]
    row_id = lax.broadcasted_iota(jnp.int32, (tokens, tokens), 0)
    col_id = lax.broadcasted_iota(jnp.int32, (tokens, tokens), 1)
    low = (row_id >= col_id).astype(F32)
    cum_col = mm_nt(low, rows[...], HIGHEST)
    cum_row = mm_nt(rows[...], low, HIGHEST)
    betas = mm_nt((row_id == col_id).astype(F32), rows[...], HIGHEST)

    def first_round(j):
        for part in range(2):
            block = kv.at[y_of(j), z, part]
            remote(block, block, kv_send.at[j, part], kv_recv.at[j, part], at(y + 1, z, x)).wait_recv()
        upward(y_of(j), 0).start()
        downward(y_of(j), 0).start()

    def forward_both(j, hop):
        arrive_up(j, hop)
        upward(j, hop).start()
        arrive_down(j, hop)
        downward(j, hop).start()

    def of_group(index):
        return at(y, g * 2 + (index % GROUP) // 2, (index % GROUP) % 2)

    def pair_copy(h):
        d = (h - r + GROUP) % GROUP
        return remote(ab_send.at[h], ab_recv.at[r], c_send.at[0, d], c_recv.at[0, d], of_group(h))

    for h in range(HEADS):
        delta_head(h, dq, dk, dv, betas, cum_col, cum_row, oloc, qeff, ab_send)
        pl.when(r != h)(lambda: pair_copy(h).start())
        if h:
            first_round(h)

    def pairs_in():
        for d in (1, 2, 3):
            block = ab_recv.at[(r - d + GROUP) % GROUP]
            remote(block, block, c_send.at[0, d], c_recv.at[0, d], of_group(r + 1)).wait_recv()

    def exchange(level, buf, mine, device):
        return [
            remote(buf.at[mine], buf.at[mine], c_send.at[level, d], c_recv.at[level, d], device(d))
            for d in (1, 2, 3)
        ]

    def exchange_in(level, buf, mine, device):
        for d in (1, 2, 3):
            block = buf.at[(mine - d + GROUP) % GROUP]
            remote(block, block, c_send.at[level, d], c_recv.at[level, d], device(d)).wait_recv()

    def fold(buf):
        a, b = [buf[i, 0] for i in range(GROUP)], [buf[i, 1].astype(F32) for i in range(GROUP)]

        def join(one, two):
            both = mm(jnp.concatenate([one[0].astype(BF16), one[1].astype(BF16)], axis=0), two[0])
            return both[:HD], both[HD:] + two[1]

        pairs = list(zip(a, b))
        early, late = join(pairs[0], pairs[1]), join(pairs[2], pairs[3])
        first = (a[0].astype(F32), b[0])
        return [first, early, join(early, pairs[2])], join(early, late)

    in_chain = lambda d: at(y, z + 2 * d, x)
    in_column = lambda d: at(y + d, z, x)

    def level_one():
        pairs_in()
        before, (a, b) = fold(ab_recv)
        for i, (ea, eb) in enumerate(before):
            e_buf[i, 0] = ea
            e_buf[i, 1] = eb
        t_buf[g, 0] = a.astype(BF16)
        t_buf[g, 1] = b.astype(BF16)
        for copy in exchange(1, t_buf, g, in_chain):
            copy.start()

    def level_two():
        exchange_in(1, t_buf, g, in_chain)
        before, (a, b) = fold(t_buf)
        eye = (row_id == col_id)[:HD, :HD].astype(F32)
        fa, fb = eye, jnp.zeros((HD, HD), F32)
        for i, (ea, eb) in enumerate(before):
            fa = jnp.where(g == i + 1, ea, fa)
            fb = jnp.where(g == i + 1, eb, fb)
        e_buf[3, 0] = fa
        e_buf[3, 1] = fb
        u_buf[y, 0] = a.astype(BF16)
        u_buf[y, 1] = b.astype(BF16)
        for copy in exchange(2, u_buf, y, in_column):
            copy.start()

    def states_out():
        copies = []
        for d in (1, 2, 3):
            to = (r + d) % GROUP
            copies.append(remote(s_send.at[to], sin.at[r], c_send.at[3, d], c_recv.at[3, d], of_group(to)))
        return copies

    def level_three():
        exchange_in(2, u_buf, y, in_column)
        state = jnp.zeros((HD, HD), F32)
        b = u_buf[0, 1].astype(F32)
        for i in range(1, NY):
            state = jnp.where(y == i, b, state)
            if i < NY - 1:
                b = mm(b, u_buf[i, 0]) + u_buf[i, 1].astype(F32)
        state = mm(state, e_buf[3, 0]) + e_buf[3, 1]
        s_send[0] = state.astype(BF16)
        for i in range(3):
            s_send[i + 1] = (mm(state, e_buf[i, 0]) + e_buf[i, 1]).astype(BF16)
        for copy in states_out():
            copy.start()
        sin[r] = s_send[r]

    def states_in():
        for d in (1, 2, 3):
            block = sin.at[(r - d + GROUP) % GROUP]
            remote(block, block, c_send.at[3, d], c_recv.at[3, d], of_group(r + 1)).wait_recv()

    def weight_cols(device):
        return weight.at[:, pl.ds(pl.multiple_of(device * cols, HD), cols)]

    def weights_out():
        own_w.start()
        for d in (1, 2, 3):
            to = (me + d) % 4
            copy = remote(weight_cols(to), wcol.at[me], w_send.at[d], w_recv.at[d], {"head": to})
            copy.start()
            sent.append(copy)

    own_w = pltpu.make_async_copy(weight_cols(me), wcol.at[me], own_sem.at[3])
    ab_recv[r] = ab_send[r]
    weights_out()
    for yk in range(NY):
        forward_both(yk, 1)

    m_ref[...] = jnp.full_like(m_ref, NEG)
    l_ref[...] = jnp.zeros_like(l_ref)
    acc_ref[...] = jnp.zeros_like(acc_ref)
    own_k.wait()
    own_v.wait()
    own_q.wait()
    for d in range(4):
        for dx in range(2):
            if d or dx:
                block = qg.at[(y + d) % NY, q_rows(x + dx)]
                remote(block, block, q_send.at[d, dx], q_recv.at[d, dx], at(y + d, z, x + dx)).wait_recv()

    for t in range(NY):
        qt[:, t * wide : (t + 1) * wide] = qg[t].T

    def attend_later(yk, k, v):
        for case in range(NY - 1):

            @pl.when(yk == case)
            def _():
                attend(case + 1, NY - 1 - case, k(), v(), qt, m_ref, l_ref, acc_ref)

    def attend_single(yk, zk):
        attend_later(yk, lambda: kv[yk, zk, 0], lambda: kv[yk, zk, 1])

    def attend_same(yk, zk):
        @pl.when(zk < z)
        def _():
            attend(yk, 1, kv[yk, zk, 0], kv[yk, zk, 1], qt, m_ref, l_ref, acc_ref)

    @pl.loop(0, NY)
    def _(yk):
        attend_single(yk, z)
        key_at = lax.broadcasted_iota(jnp.int32, (tokens, wide), 0) + x * tokens
        seen = key_at <= lax.broadcasted_iota(jnp.int32, (tokens, wide), 1)
        attend(yk, 1, kv[yk, z, 0], kv[yk, z, 1], qt, m_ref, l_ref, acc_ref, seen)

    stages = {0: level_one, 6: level_two, 9: level_three}

    @pl.loop(0, 12)
    def _(n):
        yk, hop = n % NY, n // NY + 1
        for when, stage in stages.items():
            pl.when(n == when)(stage)
        before, after = (z - hop + NZ) % NZ, (z + hop) % NZ

        @pl.when((n >= 6) & (n < 10))
        def _():
            early = n - 6
            arrive_up(early, 3)
            pl.when(early % 2 == 0)(lambda: upward(early, 3).start())
            arrive_down(early, 3)
            pl.when(early % 2 == 1)(lambda: downward(early, 3).start())

        attend_later(
            yk,
            lambda: jnp.concatenate([kv[yk, before, 0], kv[yk, after, 0]], axis=0),
            lambda: jnp.concatenate([kv[yk, before, 1], kv[yk, after, 1]], axis=0),
        )
        attend_same(yk, before)
        attend_same(yk, after)

        @pl.when(hop == 1)
        def _():
            forward_both(yk, 2)

    def tile_copies(t):
        d = (t - y + NY) % NY
        for xx in range(NX):
            dx, to, back = (xx - x + NX) % NX, at(t, z, xx), (NY - d) % NY
            rows_of = slice(xx * tokens, (xx + 1) * tokens)
            elsewhere = (t != y) | (xx != x)
            yield elsewhere, (
                remote(o.at[t, rows_of], o_recv.at[y, x], o_send_sem.at[d, dx], o_recv_sem.at[back, dx], to),
                remote(lse.at[t], lse_recv.at[y, x], l_send_sem.at[d, dx], l_recv_sem.at[back, dx], to),
            )

    opposite = (z + 4) % NZ
    for t in range(NY):
        (arrive_up if t % 2 == 0 else arrive_down)(t, 4)
        if t < NY - 1:
            attend(t + 1, NY - 1 - t, kv[t, opposite, 0], kv[t, opposite, 1], qt, m_ref, l_ref, acc_ref)
        attend_same(t, opposite)
        tile = slice(t * wide, (t + 1) * wide)
        total = l_ref[:, tile]
        some = total > 0.0
        safe = jnp.where(some, total, 1.0)
        o[t] = (acc_ref[:, tile] * (1.0 / safe)).T.astype(BF16)
        level = jnp.where(some, m_ref[:, tile] * (SCALE * LOG2E) + jnp.log2(safe), NEG)
        lse[t] = jnp.broadcast_to(level, (8, wide))
        for elsewhere, copies in tile_copies(t):

            @pl.when(elsewhere)
            def _():
                for copy in copies:
                    copy.start()

    o_recv[y, x] = o[y, q_rows(x), :]
    lse_recv[y, x] = lse[y]

    states_in()
    for h in range(HEADS):
        col = slice(h * HD, (h + 1) * HD)
        raw = mm_nt(qeff[:, col], sin[h]) + oloc[:, col]
        scaled = raw * lax.rsqrt(jnp.mean(raw * raw, axis=-1, keepdims=True) + EPSILON)
        normed[h] = scaled * dgain[...]

    first_half = lax.broadcasted_iota(jnp.int32, (8, wide), 0) < 4

    def piece_of(device, j):
        return comb.at[device, :, head_cols(y_of(j))]

    for j in range(NY):
        d = Y_ORDER[j]
        h = (y + d) % NY
        for dx in range(2):
            if d or dx:
                there = (x + dx) % NX
                block = o_recv.at[h, there]
                remote(block, block, o_send_sem.at[d, dx], o_recv_sem.at[d, dx], at(h, z, there)).wait_recv()
                block = lse_recv.at[h, there]
                remote(block, block, l_send_sem.at[d, dx], l_recv_sem.at[d, dx], at(h, z, there)).wait_recv()
        a, b = lse_recv[h, 0], lse_recv[h, 1]
        top = jnp.maximum(a, b)
        a, b = jnp.exp2(a - top), jnp.exp2(b - top)
        shares = (jnp.where(first_half, a, b) / (a + b)).T
        shares = jnp.where(x == 0, shares[:tokens], shares[tokens:])
        raw = o_recv[h, 0].astype(F32) * shares[:, :1] + o_recv[h, 1].astype(F32) * shares[:, 4:5]
        scaled = raw * lax.rsqrt(jnp.mean(raw * raw, axis=-1, keepdims=True) + EPSILON)
        comb[me, :, head_cols(h)] = (0.5 * (normed[h] + scaled * again[...])).astype(BF16)
        for way, to in enumerate((facing, sibling)):
            copy = remote(piece_of(me, j), piece_of(me, j), ag_send.at[way, j], ag_recv.at[way, j], {"head": to})
            copy.start()
            sent.append(copy)

    def share(device):
        return jnp.dot(comb[device], wcol[device], preferred_element_type=F32)

    for j in range(NY):
        block = piece_of(facing, j)
        remote(block, block, ag_send.at[0, j], ag_recv.at[0, j], {"head": facing}).wait_recv()
        copy = remote(block, block, relay_send.at[j], relay_recv.at[j], {"head": sibling})
        copy.start()
        sent.append(copy)
    own_w.wait()
    for d in (1, 2, 3):
        block = wcol.at[(me - d + 4) % 4]
        remote(block, block, w_send.at[d], w_recv.at[d], {"head": (me + d) % 4}).wait_recv()
    total = share(me) + share(facing)
    for j in range(NY):
        block = piece_of(sibling, j)
        remote(block, block, ag_send.at[1, j], ag_recv.at[1, j], {"head": sibling}).wait_recv()
    total = total + share(sibling)
    for j in range(NY):
        block = piece_of(diagonal, j)
        remote(block, block, relay_send.at[j], relay_recv.at[j], {"head": sibling}).wait_recv()
    out[...] = total + share(diagonal)
    for d in (1, 2, 3):
        pair_copy((r + d) % GROUP).wait_send()
    for t in range(NY):
        for elsewhere, copies in tile_copies(t):

            @pl.when(elsewhere)
            def _():
                for copy in copies:
                    copy.wait_send()

    for copy in sent + exchange(1, t_buf, g, in_chain) + exchange(2, u_buf, y, in_column) + states_out():
        copy.wait_send()
    for j in range(NY):
        for hop in range(4):
            if hop < UP_HOPS[j]:
                upward(j, hop).wait_send()
            if hop < DOWN_HOPS[j]:
                downward(j, hop).wait_send()


VMEM = pl.BlockSpec(memory_space=pltpu.VMEM)
ANY = pl.BlockSpec(memory_space=pl.ANY)
DMA = pltpu.SemaphoreType.DMA
LIMIT = 60 * 1024 * 1024


def local(
    hidden_in, delta_q, delta_k, delta_v, beta, log_decay, resets,
    attn_q, attn_k, attn_v, delta_gain, attn_gain, out_weight,
):
    tokens, cols = delta_q.shape
    struct = jax.ShapeDtypeStruct
    wide = NX * tokens
    vmem = pltpu.VMEM
    shared = pl.pallas_call(
        main_kernel,
        out_shape=struct((tokens, cols), F32),
        in_specs=[ANY] * 12,
        out_specs=VMEM,
        scratch_shapes=[
            vmem((NY, wide, HD), BF16),
            vmem((NY, 8, wide), F32),
            vmem((HEADS, HD, HD), BF16),
            vmem((tokens, cols), F32),
            vmem((tokens, cols), BF16),
            vmem((1, HD), F32),
            vmem((1, HD), F32),
            vmem((HEADS, tokens, HD), F32),
            vmem((NY, NX, tokens, HD), BF16),
            vmem((NY, NX, 8, wide), F32),
            vmem((4, tokens, cols), BF16),
            vmem((4, cols, cols), BF16),
            vmem((tokens, cols), BF16), vmem((tokens, cols), BF16), vmem((tokens, cols), BF16),
            vmem((HEADS, tokens), F32), vmem((HEADS, tokens), F32), vmem((1, tokens), jnp.int32),
            vmem((16, tokens), F32),
            vmem((NY, NZ, 2, tokens, HD), BF16),
            vmem((NY, wide, HD), BF16),
            vmem((HD, NY * wide), BF16),
            vmem((1, NY * wide), F32),
            vmem((1, NY * wide), F32),
            vmem((HD, NY * wide), F32),
            vmem((HEADS, 2, HD, HD), BF16),
            vmem((GROUP, 2, HD, HD), BF16),
            vmem((GROUP, 2, HD, HD), BF16),
            vmem((NY, 2, HD, HD), BF16),
            vmem((4, 2, HD, HD), F32),
            vmem((GROUP, HD, HD), BF16),
            DMA((8,)),
            DMA((4,)),
            DMA((4, 2)), DMA((4, 2)),
            DMA((4, 2)), DMA((4, 2)),
            DMA((4, 4)), DMA((4, 4)),
            DMA((4, 4)), DMA((4, 4)),
            DMA((4, 4)), DMA((4, 4)),
            DMA((4, 2)), DMA((4, 2)),
            DMA((4, 2)), DMA((4, 2)),
            DMA((4,)), DMA((4,)),
            DMA((2, 4)), DMA((2, 4)),
            DMA((4,)), DMA((4,)),
        ],
        compiler_params=pltpu.CompilerParams(
            collective_id=0, has_side_effects=True, vmem_limit_bytes=LIMIT
        ),
    )(
        delta_q, delta_k, delta_v, beta.T, log_decay.T, resets.reshape(1, tokens),
        attn_q, attn_k, attn_v, out_weight,
        delta_gain.reshape(1, HD), attn_gain.reshape(1, HD),
    )
    return (hidden_in.astype(F32) + shared).astype(BF16)


def solution(mesh):
    by_head = P("seq", "head")
    placed = (by_head,) * 6 + (P("seq"),) + (by_head,) * 3 + (P(), P(), P("head", None))
    return jax.shard_map(local, mesh=mesh, in_specs=placed, out_specs=by_head, check_vma=False)
```

```python
import jax
import jax.numpy as jnp
from jax import lax
from jax.experimental import pallas as pl
from jax.experimental.pallas import tpu as pltpu
from jax.sharding import PartitionSpec as P

HD = 128
EPSILON = 1e-06
NY, NZ, NX = 4, 8, 2
HEADS = 4
GROUP = 4
SUB = 64
MESH = pl.DeviceIdType.MESH
HIGHEST = lax.Precision.HIGHEST
F32 = jnp.float32
BF16 = jnp.bfloat16
NEG = -1e30
SCALE = HD**-0.5
LOG2E = 1.4426950408889634
Y_ORDER = (0, 1, 3, 2)
UP_HOPS = (4, 3, 4, 3)
DOWN_HOPS = (3, 4, 3, 4)


def mm(a, b):
    return jnp.dot(a.astype(BF16), b.astype(BF16), preferred_element_type=F32)


def mm_nt(a, b, precision=None):
    return lax.dot_general(
        a, b, (((1,), (1,)), ((), ())), precision=precision, preferred_element_type=F32
    )


def mm_tn(a, b):
    return lax.dot_general(
        a.astype(BF16), b.astype(BF16), (((0,), (0,)), ((), ())), preferred_element_type=F32
    )


def place():
    s = lax.axis_index("seq")
    return s // (NZ * NX), (s // NX) % NZ, s % NX


def at(y, z, x):
    return {"seq": ((y % NY) * NZ + z % NZ) * NX + x % NX}


def remote(src, dst, send, recv, device):
    return pltpu.make_async_remote_copy(
        src_ref=src,
        dst_ref=dst,
        send_sem=send,
        recv_sem=recv,
        device_id=device,
        device_id_type=MESH,
    )


def delta_head(h, dq, dk, dv, betas, cum_col, cum_row, oloc, qeff, ab_send):
    tokens = dq.shape[0]
    col = slice(h * HD, (h + 1) * HD)
    q = dq[:, col].astype(F32)
    k = dk[:, col].astype(F32)
    v = dv[:, col].astype(F32)
    q = q * (lax.rsqrt(jnp.sum(q * q, axis=-1, keepdims=True) + EPSILON) * SCALE)
    k = k * lax.rsqrt(jnp.sum(k * k, axis=-1, keepdims=True) + EPSILON)
    strength = betas[:, h + 8 : h + 9]
    row_id = lax.broadcasted_iota(jnp.int32, (tokens, tokens), 0)
    col_id = lax.broadcasted_iota(jnp.int32, (tokens, tokens), 1)
    c_col, n_col = cum_col[:, h : h + 1], cum_col[:, HEADS : HEADS + 1]
    c_row, n_row = cum_row[h : h + 1, :], cum_row[HEADS : HEADS + 1, :]
    reach = jnp.where(n_col < 0.5, jnp.exp(c_col), 0.0)
    same = (jnp.abs(n_col - n_row) < 0.5) & (row_id >= col_id)
    ratios = jnp.where(same, jnp.exp(jnp.minimum(c_col - c_row, 0.0)), 0.0)
    kb = k.astype(BF16)
    inner = mm_nt(kb, kb)
    system = jnp.where(row_id > col_id, strength * ratios * inner, 0.0)
    near = (row_id // SUB) == (col_id // SUB)
    power = jnp.where(near, -system, 0.0)
    far = jnp.where(near, 0.0, system)
    inverse = jnp.where(row_id == col_id, 1.0, power)
    reached = 2
    while reached < SUB:
        power = mm(power, power)
        inverse = inverse + mm(inverse, power)
        reached *= 2
    right = jnp.concatenate([strength * v, (strength * reach) * k], axis=1)
    solved = mm(inverse, right)
    spread = mm(inverse, far)
    total = solved
    for _ in range((tokens + SUB - 1) // SUB - 1):
        total = solved - mm(spread, total)
    n_last, c_last = n_col[tokens - 1 :, :], c_col[tokens - 1 :, :]
    tail = jnp.where(jnp.abs(n_col - n_last) < 0.5, jnp.exp(jnp.minimum(c_last - c_col, 0.0)), 0.0) * k
    moved = mm_tn(total, tail)
    eye = (row_id == col_id)[:HD, :HD]
    ab_send[h, 0] = (jnp.where(eye, reach[tokens - 1 :, :], 0.0) - moved[HD:]).astype(BF16)
    ab_send[h, 1] = moved[:HD].astype(BF16)
    seen = mm(mm_nt(q.astype(BF16), kb) * ratios, total)
    oloc[:, col] = seen[:, :HD]
    qeff[:, col] = (reach * q - seen[:, HD:]).astype(BF16)


def attend(first, tiles, k, v, q, m_ref, l_ref, acc_ref, seen=None):
    factor = SCALE * LOG2E
    wide = q.shape[1] // NY
    span = tiles * wide
    at_ = pl.ds(first * wide, span) if isinstance(first, int) else pl.ds(pl.multiple_of(first * wide, HD), span)
    s = jnp.dot(k, q[:, at_], preferred_element_type=F32)
    if seen is not None:
        s = jnp.where(seen, s, NEG)
    old = m_ref[:, at_]
    new = jnp.maximum(old, jnp.max(s, axis=0, keepdims=True))
    p = jnp.exp2((s - new) * factor)
    if seen is not None:
        p = jnp.where(seen, p, 0.0)
    shrink = jnp.exp2((old - new) * factor)
    l_ref[:, at_] = l_ref[:, at_] * shrink + jnp.sum(p, axis=0, keepdims=True)
    acc_ref[:, at_] = acc_ref[:, at_] * shrink + mm_tn(v, p)
    m_ref[:, at_] = new


def main_kernel(
    dq_in, dk_in, dv_in, beta_in, decay_in, resets_in, aq, ak, av, weight, dgain_in, again_in,
    out,
    o, lse, sin, oloc, qeff, dgain, again, normed, o_recv, lse_recv, comb, wcol,
    dq, dk, dv, beta, decay, resets, rows,
    kv, qg, qt, m_ref, l_ref, acc_ref,
    ab_send, ab_recv, t_buf, u_buf, e_buf, s_send,
    in_sem, own_sem, kv_send, kv_recv, q_send, q_recv, up_send, up_recv, down_send, down_recv,
    c_send, c_recv,
    o_send_sem, o_recv_sem, l_send_sem, l_recv_sem, w_send, w_recv, ag_send, ag_recv, relay_send, relay_recv,
):
    y, z, x = place()
    me = lax.axis_index("head")
    sibling, facing = me + 1 - 2 * (me % 2), (me + 2) % 4
    diagonal = (sibling + 2) % 4
    cols = dq.shape[1]
    r, g = (z % 2) * 2 + x, z // 2
    tokens = dq.shape[0]
    wide = NX * tokens
    loads = [
        pltpu.make_async_copy(a, b, in_sem.at[i])
        for i, (a, b) in enumerate(
            zip(
                (dq_in, dk_in, dv_in, beta_in, decay_in, resets_in, dgain_in, again_in),
                (dq, dk, dv, beta, decay, resets, dgain, again),
            )
        )
    ]
    for load in loads:
        load.start()
    across = z + 1 - 2 * (z % 2)
    beyond = z - 1 + 2 * (z % 2)
    peers = [at(y + d, z, x) for d in (1, 2, 3)]
    peers += [at(y + d, z, x + 1) for d in range(4)]
    peers += [at(y, across, x), at(y, across, x + 1), at(y, beyond, x)]
    peers += [at(y, z + d, x) for d in (2, 4, 6)]
    peers += [{"head": (me + d) % 4} for d in (1, 2, 3)]
    barrier = pltpu.get_barrier_semaphore()
    for peer in peers:
        pl.semaphore_signal(barrier, inc=1, device_id=peer, device_id_type=MESH)
    pl.semaphore_wait(barrier, len(peers))
    sent = []

    def head_cols(h):
        return pl.ds(pl.multiple_of((h % NY) * HD, HD), HD)

    def q_rows(xx):
        return pl.ds(pl.multiple_of((xx % NX) * tokens, 64), tokens)

    own_k = pltpu.make_async_copy(ak.at[:, head_cols(y)], kv.at[y, z, 0], own_sem.at[0])
    own_v = pltpu.make_async_copy(av.at[:, head_cols(y)], kv.at[y, z, 1], own_sem.at[1])
    own_q = pltpu.make_async_copy(aq.at[:, head_cols(y)], qg.at[y, q_rows(x)], own_sem.at[2])
    for send, recv, dz in ((up_send, up_recv, 1), (down_send, down_recv, NZ - 1)):
        for part, source in enumerate((ak, av)):
            remote(
                source.at[:, head_cols(y)], kv.at[y, z, part], send.at[y, 0], recv.at[y, 0], at(y, z + dz, x)
            ).start()
    own_k.start()
    own_v.start()
    for j in (1, 2, 3):
        to = y - Y_ORDER[j] + NY
        for part, source in enumerate((ak, av)):
            copy = remote(
                source.at[:, head_cols(to)], kv.at[y, z, part],
                kv_send.at[j, part], kv_recv.at[j, part], at(to, z, x),
            )
            copy.start()
            sent.append(copy)

    def y_of(j):
        return (y + Y_ORDER[j]) % NY

    def upward(j, hop):
        block = kv.at[j, (z - hop + NZ) % NZ]
        return remote(block, block, up_send.at[j, hop], up_recv.at[j, hop], at(y, z + 1, x))

    def downward(j, hop):
        block = kv.at[j, (z + hop) % NZ]
        return remote(block, block, down_send.at[j, hop], down_recv.at[j, hop], at(y, z - 1 + NZ, x))

    def arrive_up(j, hop):
        block = kv.at[j, (z - hop + NZ) % NZ]
        remote(block, block, up_send.at[j, hop - 1], up_recv.at[j, hop - 1], at(y, z + 1, x)).wait_recv()

    def arrive_down(j, hop):
        block = kv.at[j, (z + hop) % NZ]
        remote(block, block, down_send.at[j, hop - 1], down_recv.at[j, hop - 1], at(y, z + 1, x)).wait_recv()

    own_q.start()
    for d in range(4):
        for dx in range(2):
            if d or dx:
                to = y + d
                copy = remote(
                    aq.at[:, head_cols(to)], qg.at[y, q_rows(x)],
                    q_send.at[d, dx], q_recv.at[(NY - d) % NY, dx], at(to, z, x + dx),
                )
                copy.start()
                sent.append(copy)

    for load in loads:
        load.wait()
    rows[...] = jnp.zeros_like(rows)
    rows[0:HEADS] = decay[...]
    rows[HEADS : HEADS + 1] = resets[...].astype(F32)
    rows[8 : 8 + HEADS] = beta[...]
    row_id = lax.broadcasted_iota(jnp.int32, (tokens, tokens), 0)
    col_id = lax.broadcasted_iota(jnp.int32, (tokens, tokens), 1)
    low = (row_id >= col_id).astype(F32)
    cum_col = mm_nt(low, rows[...], HIGHEST)
    cum_row = mm_nt(rows[...], low, HIGHEST)
    betas = mm_nt((row_id == col_id).astype(F32), rows[...], HIGHEST)

    def first_round(j):
        for part in range(2):
            block = kv.at[y_of(j), z, part]
            remote(block, block, kv_send.at[j, part], kv_recv.at[j, part], at(y + 1, z, x)).wait_recv()
        upward(y_of(j), 0).start()
        downward(y_of(j), 0).start()

    def forward_both(j, hop):
        arrive_up(j, hop)
        upward(j, hop).start()
        arrive_down(j, hop)
        downward(j, hop).start()

    def of_group(index):
        return at(y, g * 2 + (index % GROUP) // 2, (index % GROUP) % 2)

    def pair_copy(h):
        d = (h - r + GROUP) % GROUP
        return remote(ab_send.at[h], ab_recv.at[r], c_send.at[0, d], c_recv.at[0, d], of_group(h))

    for h in range(HEADS):
        if h:
            first_round(h)
        delta_head(h, dq, dk, dv, betas, cum_col, cum_row, oloc, qeff, ab_send)
        pl.when(r != h)(lambda: pair_copy(h).start())

    def pairs_in():
        for d in (1, 2, 3):
            block = ab_recv.at[(r - d + GROUP) % GROUP]
            remote(block, block, c_send.at[0, d], c_recv.at[0, d], of_group(r + 1)).wait_recv()

    def exchange(level, buf, mine, device):
        return [
            remote(buf.at[mine], buf.at[mine], c_send.at[level, d], c_recv.at[level, d], device(d))
            for d in (1, 2, 3)
        ]

    def exchange_in(level, buf, mine, device):
        for d in (1, 2, 3):
            block = buf.at[(mine - d + GROUP) % GROUP]
            remote(block, block, c_send.at[level, d], c_recv.at[level, d], device(d)).wait_recv()

    def fold(buf):
        a, b = [buf[i, 0] for i in range(GROUP)], [buf[i, 1].astype(F32) for i in range(GROUP)]

        def join(one, two):
            both = mm(jnp.concatenate([one[0].astype(BF16), one[1].astype(BF16)], axis=0), two[0])
            return both[:HD], both[HD:] + two[1]

        pairs = list(zip(a, b))
        early, late = join(pairs[0], pairs[1]), join(pairs[2], pairs[3])
        first = (a[0].astype(F32), b[0])
        return [first, early, join(early, pairs[2])], join(early, late)

    in_chain = lambda d: at(y, z + 2 * d, x)
    in_column = lambda d: at(y + d, z, x)

    def level_one():
        pairs_in()
        before, (a, b) = fold(ab_recv)
        for i, (ea, eb) in enumerate(before):
            e_buf[i, 0] = ea
            e_buf[i, 1] = eb
        t_buf[g, 0] = a.astype(BF16)
        t_buf[g, 1] = b.astype(BF16)
        for copy in exchange(1, t_buf, g, in_chain):
            copy.start()

    def level_two():
        exchange_in(1, t_buf, g, in_chain)
        before, (a, b) = fold(t_buf)
        eye = (row_id == col_id)[:HD, :HD].astype(F32)
        fa, fb = eye, jnp.zeros((HD, HD), F32)
        for i, (ea, eb) in enumerate(before):
            fa = jnp.where(g == i + 1, ea, fa)
            fb = jnp.where(g == i + 1, eb, fb)
        e_buf[3, 0] = fa
        e_buf[3, 1] = fb
        u_buf[y, 0] = a.astype(BF16)
        u_buf[y, 1] = b.astype(BF16)
        for copy in exchange(2, u_buf, y, in_column):
            copy.start()

    def states_out():
        copies = []
        for d in (1, 2, 3):
            to = (r + d) % GROUP
            copies.append(remote(s_send.at[to], sin.at[r], c_send.at[3, d], c_recv.at[3, d], of_group(to)))
        return copies

    def level_three():
        exchange_in(2, u_buf, y, in_column)
        state = jnp.zeros((HD, HD), F32)
        b = u_buf[0, 1].astype(F32)
        for i in range(1, NY):
            state = jnp.where(y == i, b, state)
            if i < NY - 1:
                b = mm(b, u_buf[i, 0]) + u_buf[i, 1].astype(F32)
        state = mm(state, e_buf[3, 0]) + e_buf[3, 1]
        s_send[0] = state.astype(BF16)
        for i in range(3):
            s_send[i + 1] = (mm(state, e_buf[i, 0]) + e_buf[i, 1]).astype(BF16)
        for copy in states_out():
            copy.start()
        sin[r] = s_send[r]

    def states_in():
        for d in (1, 2, 3):
            block = sin.at[(r - d + GROUP) % GROUP]
            remote(block, block, c_send.at[3, d], c_recv.at[3, d], of_group(r + 1)).wait_recv()

    def weight_cols(device):
        return weight.at[:, pl.ds(pl.multiple_of(device * cols, HD), cols)]

    def weights_out():
        own_w.start()
        for d in (1, 2, 3):
            to = (me + d) % 4
            copy = remote(weight_cols(to), wcol.at[me], w_send.at[d], w_recv.at[d], {"head": to})
            copy.start()
            sent.append(copy)

    own_w = pltpu.make_async_copy(weight_cols(me), wcol.at[me], own_sem.at[3])
    ab_recv[r] = ab_send[r]
    weights_out()
    for yk in range(NY):
        forward_both(yk, 1)

    m_ref[...] = jnp.full_like(m_ref, NEG)
    l_ref[...] = jnp.zeros_like(l_ref)
    acc_ref[...] = jnp.zeros_like(acc_ref)
    own_k.wait()
    own_v.wait()
    own_q.wait()
    for d in range(4):
        for dx in range(2):
            if d or dx:
                block = qg.at[(y + d) % NY, q_rows(x + dx)]
                remote(block, block, q_send.at[d, dx], q_recv.at[d, dx], at(y + d, z, x + dx)).wait_recv()

    for t in range(NY):
        qt[:, t * wide : (t + 1) * wide] = qg[t].T

    def attend_later(yk, k, v):
        for case in range(NY - 1):

            @pl.when(yk == case)
            def _():
                attend(case + 1, NY - 1 - case, k(), v(), qt, m_ref, l_ref, acc_ref)

    def attend_single(yk, zk):
        attend_later(yk, lambda: kv[yk, zk, 0], lambda: kv[yk, zk, 1])

    def attend_same(yk, zk):
        @pl.when(zk < z)
        def _():
            attend(yk, 1, kv[yk, zk, 0], kv[yk, zk, 1], qt, m_ref, l_ref, acc_ref)

    @pl.loop(0, NY)
    def _(yk):
        attend_single(yk, z)
        key_at = lax.broadcasted_iota(jnp.int32, (tokens, wide), 0) + x * tokens
        seen = key_at <= lax.broadcasted_iota(jnp.int32, (tokens, wide), 1)
        attend(yk, 1, kv[yk, z, 0], kv[yk, z, 1], qt, m_ref, l_ref, acc_ref, seen)

    stages = {0: level_one, 6: level_two, 9: level_three}

    @pl.loop(0, 12)
    def _(n):
        yk, hop = n % NY, n // NY + 1
        for when, stage in stages.items():
            pl.when(n == when)(stage)
        before, after = (z - hop + NZ) % NZ, (z + hop) % NZ

        @pl.when((n >= 6) & (n < 10))
        def _():
            early = n - 6
            arrive_up(early, 3)
            pl.when(early % 2 == 0)(lambda: upward(early, 3).start())
            arrive_down(early, 3)
            pl.when(early % 2 == 1)(lambda: downward(early, 3).start())

        attend_later(
            yk,
            lambda: jnp.concatenate([kv[yk, before, 0], kv[yk, after, 0]], axis=0),
            lambda: jnp.concatenate([kv[yk, before, 1], kv[yk, after, 1]], axis=0),
        )
        attend_same(yk, before)
        attend_same(yk, after)

        @pl.when(hop == 1)
        def _():
            forward_both(yk, 2)

    def tile_copies(t):
        d = (t - y + NY) % NY
        for xx in range(NX):
            dx, to, back = (xx - x + NX) % NX, at(t, z, xx), (NY - d) % NY
            rows_of = slice(xx * tokens, (xx + 1) * tokens)
            elsewhere = (t != y) | (xx != x)
            yield elsewhere, (
                remote(o.at[t, rows_of], o_recv.at[y, x], o_send_sem.at[d, dx], o_recv_sem.at[back, dx], to),
                remote(lse.at[t], lse_recv.at[y, x], l_send_sem.at[d, dx], l_recv_sem.at[back, dx], to),
            )

    opposite = (z + 4) % NZ
    for t in range(NY):
        (arrive_up if t % 2 == 0 else arrive_down)(t, 4)
        if t < NY - 1:
            attend(t + 1, NY - 1 - t, kv[t, opposite, 0], kv[t, opposite, 1], qt, m_ref, l_ref, acc_ref)
        attend_same(t, opposite)
        tile = slice(t * wide, (t + 1) * wide)
        total = l_ref[:, tile]
        some = total > 0.0
        safe = jnp.where(some, total, 1.0)
        o[t] = (acc_ref[:, tile] * (1.0 / safe)).T.astype(BF16)
        level = jnp.where(some, m_ref[:, tile] * (SCALE * LOG2E) + jnp.log2(safe), NEG)
        lse[t] = jnp.broadcast_to(level, (8, wide))
        for elsewhere, copies in tile_copies(t):

            @pl.when(elsewhere)
            def _():
                for copy in copies:
                    copy.start()

    o_recv[y, x] = o[y, q_rows(x), :]
    lse_recv[y, x] = lse[y]

    states_in()
    for h in range(HEADS):
        col = slice(h * HD, (h + 1) * HD)
        raw = mm_nt(qeff[:, col], sin[h]) + oloc[:, col]
        scaled = raw * lax.rsqrt(jnp.mean(raw * raw, axis=-1, keepdims=True) + EPSILON)
        normed[h] = scaled * dgain[...]

    first_half = lax.broadcasted_iota(jnp.int32, (8, wide), 0) < 4

    def piece_of(device, j):
        return comb.at[device, :, head_cols(y_of(j))]

    for j in range(NY):
        d = Y_ORDER[j]
        h = (y + d) % NY
        for dx in range(2):
            if d or dx:
                there = (x + dx) % NX
                block = o_recv.at[h, there]
                remote(block, block, o_send_sem.at[d, dx], o_recv_sem.at[d, dx], at(h, z, there)).wait_recv()
                block = lse_recv.at[h, there]
                remote(block, block, l_send_sem.at[d, dx], l_recv_sem.at[d, dx], at(h, z, there)).wait_recv()
        a, b = lse_recv[h, 0], lse_recv[h, 1]
        top = jnp.maximum(a, b)
        a, b = jnp.exp2(a - top), jnp.exp2(b - top)
        shares = (jnp.where(first_half, a, b) / (a + b)).T
        shares = jnp.where(x == 0, shares[:tokens], shares[tokens:])
        raw = o_recv[h, 0].astype(F32) * shares[:, :1] + o_recv[h, 1].astype(F32) * shares[:, 4:5]
        scaled = raw * lax.rsqrt(jnp.mean(raw * raw, axis=-1, keepdims=True) + EPSILON)
        comb[me, :, head_cols(h)] = (0.5 * (normed[h] + scaled * again[...])).astype(BF16)
        for way, to in enumerate((facing, sibling)):
            copy = remote(piece_of(me, j), piece_of(me, j), ag_send.at[way, j], ag_recv.at[way, j], {"head": to})
            copy.start()
            sent.append(copy)

    def share(device):
        return jnp.dot(comb[device], wcol[device], preferred_element_type=F32)

    for j in range(NY):
        block = piece_of(facing, j)
        remote(block, block, ag_send.at[0, j], ag_recv.at[0, j], {"head": facing}).wait_recv()
        copy = remote(block, block, relay_send.at[j], relay_recv.at[j], {"head": sibling})
        copy.start()
        sent.append(copy)
    own_w.wait()
    for d in (1, 2, 3):
        block = wcol.at[(me - d + 4) % 4]
        remote(block, block, w_send.at[d], w_recv.at[d], {"head": (me + d) % 4}).wait_recv()
    total = share(me) + share(facing)
    for j in range(NY):
        block = piece_of(sibling, j)
        remote(block, block, ag_send.at[1, j], ag_recv.at[1, j], {"head": sibling}).wait_recv()
    total = total + share(sibling)
    for j in range(NY):
        block = piece_of(diagonal, j)
        remote(block, block, relay_send.at[j], relay_recv.at[j], {"head": sibling}).wait_recv()
    out[...] = total + share(diagonal)
    for d in (1, 2, 3):
        pair_copy((r + d) % GROUP).wait_send()
    for t in range(NY):
        for elsewhere, copies in tile_copies(t):

            @pl.when(elsewhere)
            def _():
                for copy in copies:
                    copy.wait_send()

    for copy in sent + exchange(1, t_buf, g, in_chain) + exchange(2, u_buf, y, in_column) + states_out():
        copy.wait_send()
    for j in range(NY):
        for hop in range(4):
            if hop < UP_HOPS[j]:
                upward(j, hop).wait_send()
            if hop < DOWN_HOPS[j]:
                downward(j, hop).wait_send()


VMEM = pl.BlockSpec(memory_space=pltpu.VMEM)
ANY = pl.BlockSpec(memory_space=pl.ANY)
DMA = pltpu.SemaphoreType.DMA
LIMIT = 60 * 1024 * 1024


def local(
    hidden_in, delta_q, delta_k, delta_v, beta, log_decay, resets,
    attn_q, attn_k, attn_v, delta_gain, attn_gain, out_weight,
):
    tokens, cols = delta_q.shape
    struct = jax.ShapeDtypeStruct
    wide = NX * tokens
    vmem = pltpu.VMEM
    shared = pl.pallas_call(
        main_kernel,
        out_shape=struct((tokens, cols), F32),
        in_specs=[ANY] * 12,
        out_specs=VMEM,
        scratch_shapes=[
            vmem((NY, wide, HD), BF16),
            vmem((NY, 8, wide), F32),
            vmem((HEADS, HD, HD), BF16),
            vmem((tokens, cols), F32),
            vmem((tokens, cols), BF16),
            vmem((1, HD), F32),
            vmem((1, HD), F32),
            vmem((HEADS, tokens, HD), F32),
            vmem((NY, NX, tokens, HD), BF16),
            vmem((NY, NX, 8, wide), F32),
            vmem((4, tokens, cols), BF16),
            vmem((4, cols, cols), BF16),
            vmem((tokens, cols), BF16), vmem((tokens, cols), BF16), vmem((tokens, cols), BF16),
            vmem((HEADS, tokens), F32), vmem((HEADS, tokens), F32), vmem((1, tokens), jnp.int32),
            vmem((16, tokens), F32),
            vmem((NY, NZ, 2, tokens, HD), BF16),
            vmem((NY, wide, HD), BF16),
            vmem((HD, NY * wide), BF16),
            vmem((1, NY * wide), F32),
            vmem((1, NY * wide), F32),
            vmem((HD, NY * wide), F32),
            vmem((HEADS, 2, HD, HD), BF16),
            vmem((GROUP, 2, HD, HD), BF16),
            vmem((GROUP, 2, HD, HD), BF16),
            vmem((NY, 2, HD, HD), BF16),
            vmem((4, 2, HD, HD), F32),
            vmem((GROUP, HD, HD), BF16),
            DMA((8,)),
            DMA((4,)),
            DMA((4, 2)), DMA((4, 2)),
            DMA((4, 2)), DMA((4, 2)),
            DMA((4, 4)), DMA((4, 4)),
            DMA((4, 4)), DMA((4, 4)),
            DMA((4, 4)), DMA((4, 4)),
            DMA((4, 2)), DMA((4, 2)),
            DMA((4, 2)), DMA((4, 2)),
            DMA((4,)), DMA((4,)),
            DMA((2, 4)), DMA((2, 4)),
            DMA((4,)), DMA((4,)),
        ],
        compiler_params=pltpu.CompilerParams(
            collective_id=0, has_side_effects=True, vmem_limit_bytes=LIMIT
        ),
    )(
        delta_q, delta_k, delta_v, beta.T, log_decay.T, resets.reshape(1, tokens),
        attn_q, attn_k, attn_v, out_weight,
        delta_gain.reshape(1, HD), attn_gain.reshape(1, HD),
    )
    return (hidden_in.astype(F32) + shared).astype(BF16)


def solution(mesh):
    by_head = P("seq", "head")
    placed = (by_head,) * 6 + (P("seq"),) + (by_head,) * 3 + (P(), P(), P("head", None))
    return jax.shard_map(local, mesh=mesh, in_specs=placed, out_specs=by_head, check_vma=False)
```
